128 devices in a mesh: dp: 16 (over z_lo, x, core), tile: 8 (over z_hi, y).
Axes of the slice: x: 4, y: 4, z: 4 (z_hi: 2, z_lo: 2; z = z_hi * 2 + z_lo), core: 2. Of those that a mesh axis runs over, the one named last changes fastest.
Arguments:
- features: bfloat16 [16, 64, 128, 640], P('dp', 'tile'), may hold values from -48 to 48
- cotangent: bfloat16 [16, 64, 128, 640], P('dp', 'tile'), may hold values from -6 to 6
- mask: int32 [16, 64, 128], P('dp', 'tile'), may hold values 0 or 1
- conv_weight: bfloat16 [3, 3, 640, 640], replicated, may hold values from -0.078125 to 0.078125
- gamma: float32 [640], replicated, may hold values from 0.1 to 1.9
- beta: float32 [640], replicated, may hold values from -3 to 3
Outputs:
- dfeatures: bfloat16 [16, 64, 128, 640], P('dp', 'tile')
- dweight: float32 [5760, 640], P('tile')
- dgains: float32 [2, 640], replicated
The draws below stay inside these ranges and needn't reach their ends.
All inputs are finite; a program needn't handle non-finite values. No bound on the sum of `mask` on one device may be relied on, other than what follows from the above.
Results may differ from the reference program's by a relative error of at most 0.0029.
Values may be sent and summed in bfloat16 or wider, within the bound.
A program may use at most 128 MiB of HBM per device.

```python
import math
import jax
import jax.numpy as jnp
from jax import lax

C = 640
G = 32
WIDTH = 128
IMAGES = 16
HEIGHT = 64


def draw_features(key, part):
    key = jax.random.fold_in(key, 11)
    noise_key, chan_key = jax.random.split(key, 2)
    shape = (IMAGES, HEIGHT, WIDTH, C)
    chan_scale = jnp.exp(jax.random.uniform(chan_key, (C,), jnp.float32, math.log(0.3), math.log(3.0)))
    row_pos = jnp.arange(HEIGHT, dtype=jnp.float32) / max(HEIGHT - 1, 1)
    noise = jax.random.truncated_normal(noise_key, -4.0, 4.0, shape, jnp.float32)
    row_scale = 0.3 * jnp.exp(math.log(10.0) * row_pos)
    values = noise * row_scale[None, :, None, None] * chan_scale
    return jnp.clip(values, -48.0, 48.0).astype(jnp.bfloat16)


def set_ends(array, stream_key, smallest, high):
    longest = array.shape.index(max(array.shape))
    spots = []
    for shift in (0, 1):
        where = [jax.random.randint(jax.random.fold_in(stream_key, axis), (), 0, length) for axis, length in enumerate(array.shape)]
        where[longest] = (where[longest] + shift) % array.shape[longest]
        spots.append(tuple(where))
    return array.at[spots[0]].set(smallest).at[spots[1]].set(high)


def level_of(key, dims, cuts, smallest, high):
    gain, own = 1.0, jax.random.fold_in(key, 6)
    for axis_at, blocks in cuts:
        heights = jnp.exp(jax.random.uniform(jax.random.fold_in(own, axis_at), (blocks,), jnp.float32, smallest / len(cuts), high / len(cuts)))
        gain = gain * jnp.repeat(heights, dims[axis_at] // blocks).reshape([-1 if axis == axis_at else 1 for axis in range(len(dims))])
    return gain


def bell_draw(stream_key, shape, spread, reach, cuts=(), held_as=jnp.bfloat16):
    values = jax.random.normal(stream_key, shape, jnp.float32) * spread
    if len(cuts) > 0:
        values = level_of(stream_key, shape, cuts, -0.22, 0.18) * values
    return jnp.clip(values, min=-reach, max=reach).astype(held_as)


def setup_inputs(seed: int = 0) -> dict:
    key_list = jax.random.split(jax.random.key(seed), 7)
    return {
        "features": draw_features(jax.random.fold_in(key_list[6], 71), 0),
        "cotangent": bell_draw(key_list[1], (IMAGES, HEIGHT, WIDTH, C), 1.0, 6.0, ((0, 16), (1, 8))),
        "mask": set_ends((jax.random.randint(key_list[2], (IMAGES, HEIGHT, WIDTH), 0, 2) < 1).astype(jnp.int32), jax.random.fold_in(key_list[2], 1), 0, 1),
        "conv_weight": bell_draw(key_list[3], (3, 3, C, C), (9 * C) ** -0.5, 0.078125),
        "gamma": jnp.clip(1.0 + 0.18 * jax.random.normal(key_list[4], (C,), jnp.float32), 0.1, 1.9),
        "beta": bell_draw(key_list[5], (C,), 0.5, 3.0, (), jnp.float32),
    }


EPSILON = 1e-05

def unfold(padded, row_count, col_count):
    pieces = [padded[offset_y:offset_y + row_count, offset_x:offset_x + col_count, :] for offset_y in range(3) for offset_x in range(3)]
    joined = jnp.concatenate(pieces, axis=-1)
    return joined.reshape(row_count * col_count, joined.shape[-1])

def unfold_channels(padded, row_count, col_count):
    pieces = [padded[offset_y:offset_y + row_count, offset_x:offset_x + col_count, :] for offset_y in range(3) for offset_x in range(3)]
    joined = jnp.stack(pieces, axis=-1)
    return joined.reshape(row_count * col_count, joined.shape[-2] * 9)

def reference(features, cotangent, mask, conv_weight, gamma, beta):
    per_group = C // G
    flipped_mat = conv_weight[::-1, ::-1].transpose(0, 1, 3, 2).astype(jnp.float32).reshape(9 * C, C)
    highest = lax.Precision.HIGHEST

    def per_image(inputs):
        image, upstream, holes = inputs
        grouped = image.astype(jnp.float32).reshape(HEIGHT, WIDTH, G, per_group)
        group_mean = lax.optimization_barrier(jnp.mean(grouped, axis=(0, 1, 3)))
        centered = grouped - group_mean[None, None, :, None]
        variance = lax.optimization_barrier(jnp.mean(centered * centered, axis=(0, 1, 3)))
        inverse = lax.rsqrt(variance + EPSILON)
        scaled_groups = centered * inverse[None, None, :, None]
        scaled = scaled_groups.reshape(HEIGHT, WIDTH, C)
        normed = scaled * gamma + beta
        active = jax.nn.silu(normed).astype(jnp.bfloat16)
        weighted = (upstream.astype(jnp.float32) * (1.0 + holes.astype(jnp.float32))[:, :, None]).astype(jnp.bfloat16)
        act_cols = unfold_channels(jnp.pad(active.astype(jnp.float32), ((1, 1), (1, 1), (0, 0))), HEIGHT, WIDTH)
        grad_rows = weighted.astype(jnp.float32).reshape(HEIGHT * WIDTH, C)
        weight_grad = jnp.dot(act_cols.T, grad_rows, precision=highest)
        grad_cols = unfold(jnp.pad(weighted.astype(jnp.float32), ((1, 1), (1, 1), (0, 0))), HEIGHT, WIDTH)
        dactive = jnp.dot(grad_cols, flipped_mat, precision=highest).reshape(HEIGHT, WIDTH, C)
        sigmoid_val = jax.nn.sigmoid(normed)
        dnormed = dactive * sigmoid_val * (1.0 + normed * (1.0 - sigmoid_val))
        gains = jnp.stack([lax.optimization_barrier(jnp.sum(dnormed * scaled, axis=(0, 1))), lax.optimization_barrier(jnp.sum(dnormed, axis=(0, 1)))])
        dscaled = (dnormed * gamma).reshape(HEIGHT, WIDTH, G, per_group)
        first_moment = lax.optimization_barrier(jnp.mean(dscaled, axis=(0, 1, 3)))
        second_moment = lax.optimization_barrier(jnp.mean(dscaled * scaled_groups, axis=(0, 1, 3)))
        dinput = inverse[None, None, :, None] * (dscaled - first_moment[None, None, :, None] - scaled_groups * second_moment[None, None, :, None])
        dinput = dinput.reshape(HEIGHT, WIDTH, C) + weighted.astype(jnp.float32)
        return (dinput.astype(jnp.bfloat16), weight_grad, gains)
    dinputs, weight_grads, gain_grads = lax.map(per_image, (features, cotangent, mask))
    return (dinputs, lax.optimization_barrier(jnp.sum(weight_grads, axis=0)), lax.optimization_barrier(jnp.sum(gain_grads, axis=0)))
```

```python
import jax
import jax.numpy as jnp
from jax import lax
from jax.experimental import pallas as pl
from jax.experimental.pallas import tpu as pltpu
from jax.sharding import PartitionSpec as P

MESH = pl.DeviceIdType.MESH
BF16 = jnp.bfloat16
F32 = jnp.float32

G = 32
EPSILON = 1e-05
C = 640
PER_GROUP = C // G
ROWS = 8
W = 128
CELLS = ROWS * W
STRIPS = 8
BLOCKS = 45
LANES = 48 * 128
K9 = 9 * C
CI = C // STRIPS
COUNT = float(ROWS * STRIPS * W * PER_GROUP)
SUB = 256


def kernel(
    x_hbm, cot_hbm, mask_ref, w_hbm, gamma_ref, beta_ref,
    df_hbm, dw_hbm, dg_ref,
    x, cot, wpad, cols, wmat, act_t, dn, dwv,
    ms, mr, s1, r1a, r1b, r1c, t2a, t2b, t2c, r2a, r2b, r2c, t3a, t3b, t3c, r3, gat,
    st, sb, gx, gxr, gz, gzr, gc, gcr,
    load_sem, w_sem, out_sem,
    st_send, st_recv, sb_send, sb_recv, halo_send, halo_recv,
    m_send, m_recv,
    a1_send, a1_recv, b1_send, b1_recv, c1_send, c1_recv,
    s2_send, s2_recv, s3_send, s3_recv,
    gat_send, gat_recv, g_send, g_recv,
):
    dp = lax.axis_index("dp")
    tile = lax.axis_index("tile")
    core = lax.rem(dp, 2)
    mx = lax.rem(lax.div(dp, 2), 4)
    zlo = lax.div(dp, 8)
    zhi = lax.div(tile, 4)
    my = lax.rem(tile, 4)
    mz = zhi * 2 + zlo
    mate = 1 - core

    def place(px, py, pz, pc):
        return {
            "dp": (lax.rem(pz, 2) * 4 + px) * 2 + pc,
            "tile": lax.div(pz, 2) * 4 + py,
        }

    def x_peer(d):
        return lax.rem(mx + d, 4)

    def y_peer(d):
        return lax.rem(my + d, 4)

    def z_peer(d):
        return lax.rem(mz + d, 4)

    def remote(src, dst, send, recv, device):
        return pltpu.make_async_remote_copy(
            src_ref=src, dst_ref=dst, send_sem=send, recv_sem=recv, device_id=device, device_id_type=MESH
        )

    on_x = [place(x_peer(d), my, mz, core) for d in (1, 2, 3)]
    on_y = [place(mx, y_peer(d), mz, core) for d in (1, 2, 3)]
    on_z = [place(mx, my, z_peer(d), core) for d in (1, 2, 3)]
    on_core = place(mx, my, mz, mate)
    on_zlo = place(mx, my, zhi * 2 + 1 - zlo, core)

    def on_tile(d):
        return {"dp": dp, "tile": lax.rem(tile + d, STRIPS)}

    load_x = pltpu.make_async_copy(x_hbm.at[0], x, load_sem.at[0])
    load_x.start()
    load_cot = pltpu.make_async_copy(cot_hbm.at[0], cot, load_sem.at[1])
    load_cot.start()
    loads_w = [
        pltpu.make_async_copy(w_hbm.at[k // 3, k % 3], wmat.at[:, k * C : (k + 1) * C], w_sem.at[k]) for k in range(9)
    ]
    for load in loads_w:
        load.start()

    barrier = pltpu.get_barrier_semaphore()
    for device in on_x + on_y + on_z + [on_core]:
        pl.semaphore_signal(barrier, inc=1, device_id=device, device_id_type=MESH)
    for d in (1, 2, 3):
        other = place(mx, y_peer(d), (1 - zhi) * 2 + zlo, core)
        pl.semaphore_signal(barrier, inc=1, device_id=other, device_id_type=MESH)

    load_x.wait()

    def add_rows(i, total):
        return total + jnp.sum(x[i].astype(F32), axis=0, keepdims=True)

    total = lax.fori_loop(0, ROWS, add_rows, jnp.zeros((1, C), F32))
    local_mean = total * (1.0 / CELLS)

    def add_squares(i, sq):
        centered = x[i].astype(F32) - local_mean
        return sq + jnp.sum(centered * centered, axis=0, keepdims=True)

    squares = lax.fori_loop(0, ROWS, add_squares, jnp.zeros((1, C), F32))
    row8 = lax.broadcasted_iota(jnp.int32, (8, C), 0)
    st[tile] = jnp.where(row8 == 0, total, jnp.where(row8 == 1, squares, 0.0))
    pl.semaphore_wait(barrier, 13)
    st_copies = [remote(st.at[tile], st.at[tile], st_send.at[d - 1], st_recv.at[d - 1], on_tile(d)) for d in range(1, 8)]
    for copy in st_copies:
        copy.start()

    load_cot.wait()
    factor = (1.0 + mask_ref[...].astype(F32)).T
    for i in range(ROWS):
        wpad[i + 1] = (cot[i].astype(F32) * factor[:, i : i + 1]).astype(BF16)
    halo = [
        remote(wpad.at[ROWS], wpad.at[0], halo_send.at[0], halo_recv.at[0], on_tile(1)),
        remote(wpad.at[1], wpad.at[ROWS + 1], halo_send.at[1], halo_recv.at[1], on_tile(7)),
    ]
    for copy in halo:
        copy.start()

    rowsw = lax.broadcasted_iota(jnp.int32, (W, C), 0)

    def spread(value, r, offsets):
        ahead = jnp.where(rowsw == W - 1, 0.0, pltpu.roll(value, W - 1, 0))
        behind = jnp.where(rowsw == 0, 0.0, pltpu.roll(value, 1, 0))
        for ox, shifted in enumerate((ahead, value, behind)):
            shifted = shifted.astype(BF16)
            for oy in offsets:
                k = oy * 3 + ox
                start = pl.multiple_of((r - 2 + oy) * W, W)
                cols[pl.ds(start, W), k * C : (k + 1) * C] = shifted

    def spread_inner(r, carry):
        spread(wpad[r].astype(F32), r, (0, 1, 2))
        return carry

    lax.fori_loop(2, ROWS, spread_inner, 0)
    spread(wpad[1].astype(F32), 1, (1, 2))
    spread(wpad[ROWS].astype(F32), ROWS, (0, 1))
    cols[:, K9:] = jnp.zeros((CELLS, LANES - K9), BF16)

    for copy in st_copies:
        copy.wait_recv()
    chan = lax.broadcasted_iota(jnp.int32, (C, 128), 0).astype(F32)
    group = lax.broadcasted_iota(jnp.int32, (C, 128), 1).astype(F32)
    member = jnp.where(jnp.floor((chan + 0.5) * (1.0 / PER_GROUP)) == group, 1.0, 0.0)
    chan_t = lax.broadcasted_iota(jnp.int32, (128, C), 1).astype(F32)
    group_t = lax.broadcasted_iota(jnp.int32, (128, C), 0).astype(F32)
    member_t = jnp.where(jnp.floor((chan_t + 0.5) * (1.0 / PER_GROUP)) == group_t, 1.0, 0.0)

    def to_groups(value):
        return jnp.dot(value, member, precision=lax.Precision.HIGHEST, preferred_element_type=F32)

    def to_channels(value):
        return jnp.dot(value, member_t, precision=lax.Precision.HIGHEST, preferred_element_type=F32)

    sums = st[0]
    for i in range(1, STRIPS):
        sums = sums + st[i]
    mean = to_channels(to_groups(sums) * (1.0 / COUNT))[0:1]
    apart = jnp.zeros((8, C), F32)
    for i in range(STRIPS):
        centered = st[i] * (1.0 / CELLS) - mean
        apart = apart + centered * centered
    spread_sq = apart[0:1] * float(CELLS) + sums[1:2]
    variance = to_groups(jnp.broadcast_to(spread_sq, (8, C))) * (1.0 / COUNT)
    inverse = to_channels(lax.rsqrt(variance + EPSILON))[0:1]
    gamma = gamma_ref[...]
    beta = beta_ref[...]

    def activate(i, carry):
        scaled = (x[i].astype(F32) - mean) * inverse
        normed = scaled * gamma + beta
        sig = jax.nn.sigmoid(normed)
        act = normed * sig
        dn[i] = sig * (1.0 + normed * (1.0 - sig))
        act_t[:, pl.ds(pl.multiple_of(i * W, W), W)] = act.T.astype(BF16)
        return carry

    lax.fori_loop(0, ROWS, activate, 0)

    for copy in halo:
        copy.wait_recv()
    spread(jnp.where(tile == 0, 0.0, wpad[0].astype(F32)), 0, (2,))
    spread(jnp.where(tile == STRIPS - 1, 0.0, wpad[ROWS + 1].astype(F32)), ROWS + 1, (0,))

    def half(owner, part, xq):
        lane = pl.multiple_of(((owner * 3 + part) * 4 + xq) * 256, 256)
        return jnp.dot(act_t[...], cols[:, pl.ds(lane, 256)], preferred_element_type=F32)

    def mate_copy(s, part):
        xq = x_peer(s + 1)
        return remote(ms.at[part, xq], mr.at[part, xq], m_send.at[s, part], m_recv.at[s, part], on_core)

    def x_copy(s):
        xq = x_peer(s + 1)
        return remote(s1.at[0, xq], r1a.at[s], a1_send.at[s], a1_recv.at[s], place(xq, my, mz, core))

    def y_copy(s, d):
        xq = x_peer(s + 1)
        src = s1.at[1, xq, :, :, y_peer(d)]
        return remote(src, r1b.at[d - 1, xq], b1_send.at[s, d - 1], b1_recv.at[s, d - 1], on_y[d - 1])

    def z_copy(s, d):
        xq = x_peer(s + 1)
        src = s1.at[2, xq, lax.rem(z_peer(d), 2), lax.div(z_peer(d), 2)]
        return remote(src, r1c.at[d - 1, xq], c1_send.at[s, d - 1], c1_recv.at[s, d - 1], on_z[d - 1])

    def grad_step(s, carry):
        xq = x_peer(s + 1)
        for part in range(3):
            result = half(mate, part, xq)
            for b in range(2):
                ms[part, xq, b] = result[:, b * 128 : (b + 1) * 128].astype(BF16).reshape(2, 4, CI, 128)
            mate_copy(s, part).start()
        for part in range(3):
            result = half(core, part, xq)
            mate_copy(s, part).wait_recv()
            for b in range(2):
                theirs = mr[part, xq, b].astype(F32)
                ours = result[:, b * 128 : (b + 1) * 128].reshape(2, 4, CI, 128)
                s1[part, xq, b] = (ours + theirs).astype(BF16)
            if part == 0:

                @pl.when(s < 3)
                def _():
                    x_copy(s).start()

            for d in (1, 2, 3):
                if part == 1:
                    y_copy(s, d).start()
                if part == 2:
                    z_copy(s, d).start()
        return carry

    lax.fori_loop(0, 4, grad_step, 0)

    for load in loads_w:
        load.wait()

    def dactive_step(i, carry):
        s0, s1_ = carry
        rows = pl.ds(pl.multiple_of(i * SUB, SUB), SUB)
        dact = lax.dot_general(
            cols[rows, :K9], wmat[...], (((1,), (1,)), ((), ())), preferred_element_type=F32
        )
        for j in range(SUB // W):
            r = i * (SUB // W) + j
            dnormed = dact[j * W : (j + 1) * W] * dn[r]
            dn[r] = dnormed
            scaled = (x[r].astype(F32) - mean) * inverse
            s0 = s0 + jnp.sum(dnormed, axis=0, keepdims=True)
            s1_ = s1_ + jnp.sum(dnormed * scaled, axis=0, keepdims=True)
        return s0, s1_

    zero = jnp.zeros((1, C), F32)
    sum0, sum1 = lax.fori_loop(0, CELLS // SUB, dactive_step, (zero, zero))
    sb[tile] = jnp.where(row8 == 0, sum1, jnp.where(row8 == 1, sum0, 0.0))
    sb_copies = [remote(sb.at[tile], sb.at[tile], sb_send.at[d - 1], sb_recv.at[d - 1], on_tile(d)) for d in range(1, 8)]
    for copy in sb_copies:
        copy.start()

    for s in range(3):
        x_copy(s).wait_recv()
    t2a[...] = s1[0, mx].astype(F32) + r1a[0].astype(F32) + r1a[1].astype(F32) + r1a[2].astype(F32)
    a2 = [
        remote(t2a.at[:, :, y_peer(d)], r2a.at[d - 1], s2_send.at[0, d - 1], s2_recv.at[0, d - 1], on_y[d - 1])
        for d in (1, 2, 3)
    ]
    for copy in a2:
        copy.start()
    for s in range(4):
        for d in (1, 2, 3):
            y_copy(s, d).wait_recv()
    for q in range(4):
        t2b[q] = (
            s1[1, q, :, :, my].astype(F32) + r1b[0, q].astype(F32) + r1b[1, q].astype(F32) + r1b[2, q].astype(F32)
        )
    b2 = [
        remote(
            t2b.at[:, lax.rem(z_peer(d), 2), lax.div(z_peer(d), 2)],
            r2b.at[d - 1], s2_send.at[1, d - 1], s2_recv.at[1, d - 1], on_z[d - 1],
        )
        for d in (1, 2, 3)
    ]
    for copy in b2:
        copy.start()
    for s in range(4):
        for d in (1, 2, 3):
            z_copy(s, d).wait_recv()
    for q in range(4):
        t2c[q] = (
            s1[2, q, zlo, zhi].astype(F32) + r1c[0, q].astype(F32) + r1c[1, q].astype(F32) + r1c[2, q].astype(F32)
        )
    c2 = [
        remote(t2c.at[x_peer(d)], r2c.at[d - 1], s2_send.at[2, d - 1], s2_recv.at[2, d - 1], on_x[d - 1])
        for d in (1, 2, 3)
    ]
    for copy in c2:
        copy.start()

    for copy in sb_copies:
        copy.wait_recv()
    gsum = sb[0]
    for i in range(1, STRIPS):
        gsum = gsum + sb[i]
    gx[...] = gsum
    g1 = [remote(gx, gxr.at[d - 1], g_send.at[d - 1], g_recv.at[d - 1], on_x[d - 1]) for d in (1, 2, 3)]
    for copy in g1:
        copy.start()
    moments = to_channels(to_groups(gsum * gamma) * (1.0 / COUNT))
    second = moments[0:1]
    first = moments[1:2]

    def finish(i, carry):
        scaled = (x[i].astype(F32) - mean) * inverse
        grad = inverse * (dn[i] * gamma - first - scaled * second) + wpad[i + 1].astype(F32)
        cot[i] = grad.astype(BF16)
        return carry

    lax.fori_loop(0, ROWS, finish, 0)
    store_df = pltpu.make_async_copy(cot, df_hbm.at[0], out_sem.at[0])
    store_df.start()

    for copy in a2:
        copy.wait_recv()
    t3a[...] = t2a[:, :, my] + r2a[0] + r2a[1] + r2a[2]
    a3 = [
        remote(
            t3a.at[lax.rem(z_peer(d), 2), lax.div(z_peer(d), 2)],
            r3.at[0, d - 1], s3_send.at[0, d - 1], s3_recv.at[0, d - 1], on_z[d - 1],
        )
        for d in (1, 2, 3)
    ]
    for copy in a3:
        copy.start()
    for copy in b2:
        copy.wait_recv()
    t3b[...] = t2b[:, zlo, zhi] + r2b[0] + r2b[1] + r2b[2]
    b3 = [
        remote(t3b.at[x_peer(d)], r3.at[1, d - 1], s3_send.at[1, d - 1], s3_recv.at[1, d - 1], on_x[d - 1])
        for d in (1, 2, 3)
    ]
    for copy in b3:
        copy.start()
    for copy in c2:
        copy.wait_recv()
    t3c[...] = t2c[mx] + r2c[0] + r2c[1] + r2c[2]
    c3 = [
        remote(t3c.at[y_peer(d)], r3.at[2, d - 1], s3_send.at[2, d - 1], s3_recv.at[2, d - 1], on_y[d - 1])
        for d in (1, 2, 3)
    ]
    for copy in c3:
        copy.start()
    for copy in g1:
        copy.wait_recv()
    gz[...] = gx[...] + gxr[0] + gxr[1] + gxr[2]
    g2 = remote(gz, gzr, g_send.at[3], g_recv.at[3], on_zlo)
    g2.start()

    for part, copies in enumerate((a3, b3, c3)):
        for copy in copies:
            copy.wait_recv()
        own = (t3a[zlo, zhi], t3b[mx], t3c[my])[part]
        gat[core, zlo, mx, part] = (own + r3[part, 0] + r3[part, 1] + r3[part, 2]).astype(BF16)

    mine = gat.at[core, zlo, mx]
    k1 = [remote(mine, mine, gat_send.at[d - 1], gat_recv.at[d - 1], on_x[d - 1]) for d in (1, 2, 3)]
    for copy in k1:
        copy.start()
    g2.wait_recv()
    gc[...] = gz[...] + gzr[...]
    g3 = remote(gc, gcr, g_send.at[4], g_recv.at[4], on_core)
    g3.start()
    for copy in k1:
        copy.wait_recv()
    quad = gat.at[core, zlo]
    k2 = remote(quad, quad, gat_send.at[3], gat_recv.at[3], on_zlo)
    k2.start()
    g3.wait_recv()
    dg_ref[...] = (gc[...] + gcr[...])[0:2]
    k2.wait_recv()
    oct_ = gat.at[core]
    k3 = remote(oct_, oct_, gat_send.at[4], gat_recv.at[4], on_core)
    k3.start()
    k3.wait_recv()
    for b in range(BLOCKS):
        c, rest = divmod(b, 24)
        part, rest = divmod(rest, 8)
        xq, zq = divmod(rest, 2)
        k, j = divmod(b, 5)
        dwv[j, pl.ds(k, CI, stride=9), :] = gat[c, zq, xq, part].astype(F32)
    stores = [pltpu.make_async_copy(dwv.at[j], dw_hbm.at[:, j * 128 : (j + 1) * 128], out_sem.at[j + 1]) for j in range(5)]
    for store in stores:
        store.start()

    for copy in st_copies + halo + sb_copies + a2 + b2 + c2 + a3 + b3 + c3 + g1 + [g2, g3] + k1 + [k2, k3]:
        copy.wait_send()

    def drain(s, carry):
        for part in range(3):
            mate_copy(s, part).wait_send()
        for d in (1, 2, 3):
            y_copy(s, d).wait_send()
            z_copy(s, d).wait_send()

        @pl.when(s < 3)
        def _():
            x_copy(s).wait_send()

        return carry

    lax.fori_loop(0, 4, drain, 0)
    store_df.wait()
    for store in stores:
        store.wait()


def shards(features, cotangent, mask, conv_weight, gamma, beta):
    anywhere = pl.BlockSpec(memory_space=pl.ANY)
    vmem = pl.BlockSpec(memory_space=pltpu.VMEM)
    dma = pltpu.SemaphoreType.DMA

    def buf(*shape, dtype=BF16):
        return pltpu.VMEM(shape, dtype)

    panel = (CI, 128)
    return pl.pallas_call(
        kernel,
        out_shape=(
            jax.ShapeDtypeStruct((1, ROWS, W, C), BF16),
            jax.ShapeDtypeStruct((9 * CI, C), F32),
            jax.ShapeDtypeStruct((2, C), F32),
        ),
        in_specs=[anywhere, anywhere, vmem, anywhere, vmem, vmem],
        out_specs=(anywhere, anywhere, vmem),
        scratch_shapes=[
            buf(ROWS, W, C),
            buf(ROWS, W, C),
            buf(ROWS + 2, W, C),
            buf(CELLS, LANES),
            buf(C, K9),
            buf(C, CELLS),
            buf(ROWS, W, C, dtype=F32),
            buf(5, 9 * CI, 128, dtype=F32),
            buf(3, 4, 2, 2, 4, *panel),
            buf(3, 4, 2, 2, 4, *panel),
            buf(3, 4, 2, 2, 4, *panel),
            buf(3, 2, 2, 4, *panel),
            buf(3, 4, 2, 2, *panel),
            buf(3, 4, 4, *panel),
            buf(2, 2, 4, *panel, dtype=F32),
            buf(4, 2, 2, *panel, dtype=F32),
            buf(4, 4, *panel, dtype=F32),
            buf(3, 2, 2, *panel, dtype=F32),
            buf(3, 4, *panel, dtype=F32),
            buf(3, 4, *panel, dtype=F32),
            buf(2, 2, *panel, dtype=F32),
            buf(4, *panel, dtype=F32),
            buf(4, *panel, dtype=F32),
            buf(3, 3, *panel, dtype=F32),
            buf(2, 2, 4, 3, *panel),
            buf(STRIPS, 8, C, dtype=F32),
            buf(STRIPS, 8, C, dtype=F32),
            buf(8, C, dtype=F32),
            buf(3, 8, C, dtype=F32),
            buf(8, C, dtype=F32),
            buf(8, C, dtype=F32),
            buf(8, C, dtype=F32),
            buf(8, C, dtype=F32),
            dma((2,)),
            dma((9,)),
            dma((6,)),
            dma((7,)),
            dma((7,)),
            dma((7,)),
            dma((7,)),
            dma((2,)),
            dma((2,)),
            dma((4, 3)),
            dma((4, 3)),
            dma((3,)),
            dma((3,)),
            dma((4, 3)),
            dma((4, 3)),
            dma((4, 3)),
            dma((4, 3)),
            dma((3, 3)),
            dma((3, 3)),
            dma((3, 3)),
            dma((3, 3)),
            dma((5,)),
            dma((5,)),
            dma((5,)),
            dma((5,)),
        ],
        compiler_params=pltpu.CompilerParams(
            collective_id=0, has_side_effects=True, vmem_limit_bytes=60 * 1024 * 1024
        ),
        cost_estimate=pl.CostEstimate(flops=4 * CELLS * K9 * C, bytes_accessed=13_000_000, transcendentals=CELLS * C),
    )(features, cotangent, mask[0], conv_weight, gamma[None], beta[None])


def solution(mesh):
    placed = (
        P("dp", "tile", None, None),
        P("dp", "tile", None, None),
        P("dp", "tile", None),
        P(),
        P(),
        P(),
    )
    return jax.shard_map(
        shards,
        mesh=mesh,
        in_specs=placed,
        out_specs=(P("dp", "tile", None, None), P("tile", None), P()),
        check_vma=False,
    )
```

```python
import jax
import jax.numpy as jnp
from jax import lax
from jax.experimental import pallas as pl
from jax.experimental.pallas import tpu as pltpu
from jax.sharding import PartitionSpec as P

MESH = pl.DeviceIdType.MESH
BF16 = jnp.bfloat16
F32 = jnp.float32

G = 32
EPSILON = 1e-05
C = 640
PER_GROUP = C // G
ROWS = 8
W = 128
CELLS = ROWS * W
STRIPS = 8
K3 = 3 * C
LANES = 2048
HALF = LANES // 2
BLOCKS = K3 // 128
K9 = 9 * C
CI = C // STRIPS
COUNT = float(ROWS * STRIPS * W * PER_GROUP)
SUB = 256


def kernel(
    x_hbm, cot_hbm, mask_ref, w_hbm, gamma_ref, beta_ref,
    df, dwv, dg_ref,
    x, cot, wpad, wpad_m, cols, cols_m, wmat, act_t, act_m, dn,
    part_sum, own1, own2, s1, r1a, r1b, r1c, t2a, t2b, t2c, h2a, h2b, h2c, r2a, r2b, r2c, t3a, t3b, t3c, r3, gat,
    st, sb, gx, gxr, gz, gzr, gc, gcr,
    load_sem, w_sem,
    st_send, st_recv, sb_send, sb_recv, halo_send, halo_recv,
    wm_send, wm_recv, am_send, am_recv, hm_send, hm_recv,
    a1_send, a1_recv, b1_send, b1_recv, c1_send, c1_recv,
    s2_send, s2_recv, s3_send, s3_recv,
    gat_send, gat_recv, fwd_send, fwd_recv, g_send, g_recv,
):
    dp = lax.axis_index("dp")
    tile = lax.axis_index("tile")
    core = lax.rem(dp, 2)
    mx = lax.rem(lax.div(dp, 2), 4)
    zlo = lax.div(dp, 8)
    zhi = lax.div(tile, 4)
    my = lax.rem(tile, 4)
    mz = zhi * 2 + zlo
    mate = 1 - core

    def place(px, py, pz, pc):
        return {
            "dp": (lax.rem(pz, 2) * 4 + px) * 2 + pc,
            "tile": lax.div(pz, 2) * 4 + py,
        }

    def x_peer(d):
        return lax.rem(mx + d, 4)

    def y_peer(d):
        return lax.rem(my + d, 4)

    def z_peer(d):
        return lax.rem(mz + d, 4)

    def remote(src, dst, send, recv, device):
        return pltpu.make_async_remote_copy(
            src_ref=src, dst_ref=dst, send_sem=send, recv_sem=recv, device_id=device, device_id_type=MESH
        )

    on_x = [place(x_peer(d), my, mz, core) for d in (1, 2, 3)]
    on_y = [place(mx, y_peer(d), mz, core) for d in (1, 2, 3)]
    on_z = [place(mx, my, z_peer(d), core) for d in (1, 2, 3)]
    on_core = place(mx, my, mz, mate)
    on_zlo = place(mx, my, zhi * 2 + 1 - zlo, core)

    def on_tile(d):
        return {"dp": dp, "tile": lax.rem(tile + d, STRIPS)}

    load_x = pltpu.make_async_copy(x_hbm.at[0], x, load_sem.at[0])
    load_x.start()
    load_cot = pltpu.make_async_copy(cot_hbm.at[0], cot, load_sem.at[1])
    load_cot.start()
    loads_w = [
        pltpu.make_async_copy(w_hbm.at[k // 3, k % 3], wmat.at[:, k * C : (k + 1) * C], w_sem.at[k]) for k in range(9)
    ]

    barrier = pltpu.get_barrier_semaphore()
    for device in on_x + on_y + on_z + [on_core]:
        pl.semaphore_signal(barrier, inc=1, device_id=device, device_id_type=MESH)
    for d in (1, 2, 3):
        other = place(mx, y_peer(d), (1 - zhi) * 2 + zlo, core)
        pl.semaphore_signal(barrier, inc=1, device_id=other, device_id_type=MESH)
        other = place(x_peer(d), my, zhi * 2 + 1 - zlo, core)
        pl.semaphore_signal(barrier, inc=1, device_id=other, device_id_type=MESH)

    load_x.wait()

    def fold(value):
        return jnp.sum(value.reshape(W // 8, 8, C), axis=0)

    zeros8 = jnp.zeros((8, C), F32)
    total = lax.fori_loop(0, ROWS, lambda i, acc: acc + fold(x[i].astype(F32)), zeros8)
    total = jnp.sum(total, axis=0, keepdims=True)
    local_mean = total * (1.0 / CELLS)

    def add_squares(i, acc):
        centered = x[i].astype(F32) - local_mean
        return acc + fold(centered * centered)

    squares = jnp.sum(lax.fori_loop(0, ROWS, add_squares, zeros8), axis=0, keepdims=True)
    st[tile, 0:1] = total
    st[tile, 1:2] = squares
    pl.semaphore_wait(barrier, 16)
    st_copies = [remote(st.at[tile], st.at[tile], st_send.at[d - 1], st_recv.at[d - 1], on_tile(d)) for d in range(1, 8)]
    for copy in st_copies:
        copy.start()

    load_cot.wait()
    for load in loads_w:
        load.start()
    factor = (1.0 + mask_ref[...].astype(F32)).T
    for i in range(ROWS):
        wpad[i + 1] = (cot[i].astype(F32) * factor[:, i : i + 1]).astype(BF16)
    halo = [
        remote(wpad.at[ROWS], wpad.at[0], halo_send.at[0], halo_recv.at[0], on_tile(1)),
        remote(wpad.at[1], wpad.at[ROWS + 1], halo_send.at[1], halo_recv.at[1], on_tile(7)),
    ]
    mate_w = remote(wpad.at[pl.ds(1, ROWS)], wpad_m.at[pl.ds(1, ROWS)], wm_send.at[0], wm_recv.at[0], on_core)
    mate_w.start()
    for copy in halo:
        copy.start()

    rowsw = lax.broadcasted_iota(jnp.int32, (W, C), 0)

    def shifts(value):
        value = value.astype(F32)
        ahead = jnp.where(rowsw == W - 1, 0.0, pltpu.roll(value, W - 1, 0))
        behind = jnp.where(rowsw == 0, 0.0, pltpu.roll(value, 1, 0))
        return ahead.astype(BF16), value.astype(BF16), behind.astype(BF16)

    def spread(r):
        rows = pl.ds(pl.multiple_of(r * W, W), W)
        for ox, shifted in enumerate(shifts(wpad[r])):
            cols[rows, ox * C : (ox + 1) * C] = shifted
        cols[rows, K3:] = jnp.zeros((W, LANES - K3), BF16)

    def spread_mate(r):
        rows = pl.ds(pl.multiple_of(r * W, W), W)
        ahead, middle, behind = shifts(wpad_m[r])
        split = HALF - C

        @pl.when(core == 0)
        def _():
            cols_m[rows, :C] = ahead
            cols_m[rows, C:] = middle[:, :split]

        @pl.when(core == 1)
        def _():
            cols_m[rows, : C - split] = middle[:, split:]
            cols_m[rows, C - split : 2 * C - split] = behind
            cols_m[rows, 2 * C - split :] = jnp.zeros((W, LANES - K3), BF16)

    def inner(step):
        def body(r, carry):
            step(r)
            return carry

        lax.fori_loop(1, ROWS + 1, body, 0)

    inner(spread)

    for copy in st_copies:
        copy.wait_recv()
    chan = lax.broadcasted_iota(jnp.int32, (C, 128), 0).astype(F32)
    group = lax.broadcasted_iota(jnp.int32, (C, 128), 1).astype(F32)
    member = jnp.where(jnp.floor((chan + 0.5) * (1.0 / PER_GROUP)) == group, 1.0, 0.0)
    chan_t = lax.broadcasted_iota(jnp.int32, (128, C), 1).astype(F32)
    group_t = lax.broadcasted_iota(jnp.int32, (128, C), 0).astype(F32)
    member_t = jnp.where(jnp.floor((chan_t + 0.5) * (1.0 / PER_GROUP)) == group_t, 1.0, 0.0)

    def to_groups(value):
        return jnp.dot(value, member, precision=lax.Precision.HIGHEST, preferred_element_type=F32)

    def to_channels(value):
        return jnp.dot(value, member_t, precision=lax.Precision.HIGHEST, preferred_element_type=F32)

    sums = st[0]
    for i in range(1, STRIPS):
        sums = sums + st[i]
    mean = to_channels(to_groups(jnp.broadcast_to(sums[0:1], (8, C))) * (1.0 / COUNT))[0:1]
    apart = jnp.zeros((1, C), F32)
    for i in range(STRIPS):
        centered = st[i, 0:1] * (1.0 / CELLS) - mean
        apart = apart + centered * centered
    spread_sq = apart * float(CELLS) + sums[1:2]
    variance = to_groups(jnp.broadcast_to(spread_sq, (8, C))) * (1.0 / COUNT)
    inverse = to_channels(lax.rsqrt(variance + EPSILON))[0:1]
    gamma = gamma_ref[...].reshape(1, C)
    beta = beta_ref[...].reshape(1, C)

    def mate_act(i):
        block = pl.ds(pl.multiple_of(i * W, W), W)
        return remote(act_t.at[:, block], act_m.at[:, block], am_send.at[i], am_recv.at[i], on_core)

    def activate(i, carry):
        scaled = (x[i].astype(F32) - mean) * inverse
        normed = scaled * gamma + beta
        sig = jax.nn.sigmoid(normed)
        act = normed * sig
        dn[i] = sig * (1.0 + normed * (1.0 - sig))
        act_t[:, pl.ds(pl.multiple_of(i * W, W), W)] = act.T.astype(BF16)
        mate_act(i).start()
        return carry

    lax.fori_loop(0, ROWS, activate, 0)

    for copy in halo:
        copy.wait_recv()

    @pl.when(tile == 0)
    def _():
        wpad[0] = jnp.zeros((W, C), BF16)

    @pl.when(tile == STRIPS - 1)
    def _():
        wpad[ROWS + 1] = jnp.zeros((W, C), BF16)

    mate_edge = [
        remote(wpad.at[r], wpad_m.at[r], hm_send.at[n], hm_recv.at[n], on_core) for n, r in enumerate((0, ROWS + 1))
    ]
    for copy in mate_edge:
        copy.start()
    spread(0)
    spread(ROWS + 1)
    mate_w.wait_recv()
    inner(spread_mate)
    for copy in mate_edge:
        copy.wait_recv()
    spread_mate(0)
    spread_mate(ROWS + 1)
    for i in range(ROWS):
        mate_act(i).wait_recv()

    def partial(part, xq):
        rows = pl.ds((2 - part) * W, CELLS)
        own = cols[rows, pl.ds(pl.multiple_of(core * HALF + xq * 256, 256), 256)]
        theirs = cols_m[rows, pl.ds(pl.multiple_of(xq * 256, 256), 256)]
        return jnp.dot(act_t[...], own, preferred_element_type=F32) + jnp.dot(
            act_m[...], theirs, preferred_element_type=F32
        )

    def turn(s):
        return jnp.where(s == 0, 1, jnp.where(s == 1, 3, jnp.where(s == 2, 2, 0)))

    def x_copy(s):
        xq = x_peer(turn(s))
        return remote(s1.at[0, xq], r1a.at[s], a1_send.at[s], a1_recv.at[s], place(xq, my, mz, core))

    def y_copy(s, d):
        xq = x_peer(turn(s))
        src = s1.at[1, xq, :, :, y_peer(d)]
        return remote(src, r1b.at[d - 1, xq], b1_send.at[s, d - 1], b1_recv.at[s, d - 1], on_y[d - 1])

    def z_copy(s, d):
        xq = x_peer(turn(s))
        src = s1.at[2, xq, lax.rem(z_peer(d), 2), lax.div(z_peer(d), 2)]
        return remote(src, r1c.at[d - 1, xq], c1_send.at[s, d - 1], c1_recv.at[s, d - 1], on_z[d - 1])

    def grad_step(s, carry):
        xq = x_peer(turn(s))
        for part in range(3):
            result = partial(part, xq)
            for b in range(2):
                part_sum[b] = result[:, b * 128 : (b + 1) * 128].reshape(2, 4, CI, 128)
            s1[part, xq] = part_sum[...].astype(BF16)
            if part == 0:

                @pl.when(s < 3)
                def _():
                    x_copy(s).start()

            for d in (1, 3, 2):
                if part == 1:
                    y_copy(s, d).start()
                if part == 2:
                    z_copy(s, d).start()
            if part == 1:
                own1[xq] = part_sum[:, :, my]
            if part == 2:
                own2[xq] = part_sum[zlo, zhi]
            if part == 0:

                @pl.when(s == 3)
                def _():
                    t2a[...] = part_sum[...]
        return carry

    lax.fori_loop(0, 4, grad_step, 0)

    for load in loads_w:
        load.wait()

    def dactive_step(i, carry):
        s0, s1_ = carry
        dact = jnp.zeros((SUB, C), F32)
        for oy in range(3):
            window = cols[pl.ds(pl.multiple_of(i * SUB + (2 - oy) * W, W), SUB), :K3]
            dact = dact + lax.dot_general(
                window, wmat[:, oy * K3 : (oy + 1) * K3], (((1,), (1,)), ((), ())), preferred_element_type=F32
            )
        for j in range(SUB // W):
            r = i * (SUB // W) + j
            dnormed = dact[j * W : (j + 1) * W] * dn[r]
            dn[r] = dnormed
            scaled = (x[r].astype(F32) - mean) * inverse
            s0 = s0 + fold(dnormed)
            s1_ = s1_ + fold(dnormed * scaled)
        return s0, s1_

    sums01 = lax.fori_loop(0, 3, dactive_step, (zeros8, zeros8))

    for s in range(3):
        x_copy(s).wait_recv()
    total = t2a[...] + r1a[0].astype(F32) + r1a[1].astype(F32) + r1a[2].astype(F32)
    t2a[...] = total
    h2a[...] = total.astype(BF16)
    a2 = [
        remote(h2a.at[:, :, y_peer(d)], r2a.at[d - 1], s2_send.at[0, d - 1], s2_recv.at[0, d - 1], on_y[d - 1])
        for d in (1, 2, 3)
    ]
    for copy in a2:
        copy.start()
    for s in range(4):
        for d in (1, 2, 3):
            y_copy(s, d).wait_recv()
    for q in range(4):
        total = own1[q] + r1b[0, q].astype(F32) + r1b[1, q].astype(F32) + r1b[2, q].astype(F32)
        t2b[q] = total
        h2b[q] = total.astype(BF16)
    b2 = [
        remote(
            h2b.at[:, lax.rem(z_peer(d), 2), lax.div(z_peer(d), 2)],
            r2b.at[d - 1], s2_send.at[1, d - 1], s2_recv.at[1, d - 1], on_z[d - 1],
        )
        for d in (1, 2, 3)
    ]
    for copy in b2:
        copy.start()
    for s in range(4):
        for d in (1, 2, 3):
            z_copy(s, d).wait_recv()
    for q in range(4):
        total = own2[q] + r1c[0, q].astype(F32) + r1c[1, q].astype(F32) + r1c[2, q].astype(F32)
        t2c[q] = total
        h2c[q] = total.astype(BF16)
    c2 = [
        remote(h2c.at[x_peer(d)], r2c.at[d - 1], s2_send.at[2, d - 1], s2_recv.at[2, d - 1], on_x[d - 1])
        for d in (1, 2, 3)
    ]
    for copy in c2:
        copy.start()

    sums01 = dactive_step(3, sums01)
    sum0 = jnp.sum(sums01[0], axis=0, keepdims=True)
    sum1 = jnp.sum(sums01[1], axis=0, keepdims=True)
    sb[tile, 0:1] = sum1
    sb[tile, 1:2] = sum0
    sb_copies = [remote(sb.at[tile], sb.at[tile], sb_send.at[d - 1], sb_recv.at[d - 1], on_tile(d)) for d in range(1, 8)]
    for copy in sb_copies:
        copy.start()

    for copy in sb_copies:
        copy.wait_recv()
    gsum = sb[0]
    for i in range(1, STRIPS):
        gsum = gsum + sb[i]
    gx[...] = gsum
    g1 = [remote(gx, gxr.at[d - 1], g_send.at[d - 1], g_recv.at[d - 1], on_x[d - 1]) for d in (1, 2, 3)]
    for copy in g1:
        copy.start()
    weighed = gsum * gamma
    row8 = lax.broadcasted_iota(jnp.int32, (8, C), 0)
    weighed = jnp.where(row8 == 0, weighed[0:1], weighed[1:2])
    moments = to_channels(to_groups(weighed) * (1.0 / COUNT))
    second = moments[0:1]
    first = moments[1:2]

    def finish(i, carry):
        scaled = (x[i].astype(F32) - mean) * inverse
        grad = inverse * (dn[i] * gamma - first - scaled * second) + wpad[i + 1].astype(F32)
        df[0, i] = grad.astype(BF16)
        return carry

    lax.fori_loop(0, ROWS, finish, 0)

    for copy in a2:
        copy.wait_recv()
    t3a[...] = t2a[:, :, my] + r2a[0].astype(F32) + r2a[1].astype(F32) + r2a[2].astype(F32)
    a3 = [
        remote(
            t3a.at[lax.rem(z_peer(d), 2), lax.div(z_peer(d), 2)],
            r3.at[0, d - 1], s3_send.at[0, d - 1], s3_recv.at[0, d - 1], on_z[d - 1],
        )
        for d in (1, 2, 3)
    ]
    for copy in a3:
        copy.start()
    for copy in b2:
        copy.wait_recv()
    t3b[...] = t2b[:, zlo, zhi] + r2b[0].astype(F32) + r2b[1].astype(F32) + r2b[2].astype(F32)
    b3 = [
        remote(t3b.at[x_peer(d)], r3.at[1, d - 1], s3_send.at[1, d - 1], s3_recv.at[1, d - 1], on_x[d - 1])
        for d in (1, 2, 3)
    ]
    for copy in b3:
        copy.start()
    for copy in c2:
        copy.wait_recv()
    t3c[...] = t2c[mx] + r2c[0].astype(F32) + r2c[1].astype(F32) + r2c[2].astype(F32)
    c3 = [
        remote(t3c.at[y_peer(d)], r3.at[2, d - 1], s3_send.at[2, d - 1], s3_recv.at[2, d - 1], on_y[d - 1])
        for d in (1, 2, 3)
    ]
    for copy in c3:
        copy.start()
    for copy in g1:
        copy.wait_recv()
    gz[...] = gx[...] + gxr[0] + gxr[1] + gxr[2]
    g2 = remote(gz, gzr, g_send.at[3], g_recv.at[3], on_zlo)
    g2.start()

    for part, copies in enumerate((a3, b3, c3)):
        for copy in copies:
            copy.wait_recv()
        own = (t3a[zlo, zhi], t3b[mx], t3c[my])[part]
        gat[core, zlo, mx, part] = (own + r3[part, 0] + r3[part, 1] + r3[part, 2]).astype(BF16)

    def piece(dz, dx):
        return gat.at[core, lax.rem(zlo + dz, 2), lax.rem(mx + 4 - dx, 4)]

    def gat_copy(dz, dx):
        mine = gat.at[core, zlo, mx]
        target = place(x_peer(dx), my, zhi * 2 + lax.rem(zlo + dz, 2), core)
        return remote(mine, mine, gat_send.at[dz * 4 + dx], gat_recv.at[dz * 4 + dx], target)

    def mate_gat(dz, dx):
        block = piece(dz, dx)
        return remote(block, block, fwd_send.at[dz * 4 + dx], fwd_recv.at[dz * 4 + dx], on_core)

    def assemble(c, dz, dx):
        zq = lax.rem(zlo + dz, 2)
        xq = lax.rem(mx + 4 - dx, 4)
        for part in range(3):
            b = c * 8 + xq * 2 + zq

            @pl.when(b < BLOCKS)
            def _():
                k = part * 3 + lax.div(b, 5)
                j = lax.rem(b, 5)
                dwv[j, pl.ds(k, CI, stride=9), :] = gat[c, zq, xq, part].astype(F32)

    order = ((0, 0), (0, 1), (0, 3), (1, 0), (0, 2), (1, 1), (1, 3), (1, 2))
    for dz, dx in order[1:]:
        gat_copy(dz, dx).start()
    mate_gat(0, 0).start()
    assemble(core, 0, 0)
    g2.wait_recv()
    gc[...] = gz[...] + gzr[...]
    g3 = remote(gc, gcr, g_send.at[4], g_recv.at[4], on_core)
    g3.start()
    for n, (dz, dx) in enumerate(order[1:]):
        gat_copy(dz, dx).wait_recv()
        mate_gat(dz, dx).start()
        assemble(core, dz, dx)
        mate_gat(*order[n]).wait_recv()
        assemble(mate, *order[n])
    g3.wait_recv()
    dg_ref[...] = gc[...] + gcr[...]
    mate_gat(*order[7]).wait_recv()
    assemble(mate, *order[7])

    for copy in st_copies + halo + [mate_w] + mate_edge + sb_copies + a2 + b2 + c2 + a3 + b3 + c3 + g1 + [g2, g3]:
        copy.wait_send()
    for dz, dx in order:
        mate_gat(dz, dx).wait_send()
        if (dz, dx) != (0, 0):
            gat_copy(dz, dx).wait_send()

    def drain(s, carry):
        mate_act(s * 2).wait_send()
        mate_act(s * 2 + 1).wait_send()
        for d in (1, 2, 3):
            y_copy(s, d).wait_send()
            z_copy(s, d).wait_send()

        @pl.when(s < 3)
        def _():
            x_copy(s).wait_send()

        return carry

    lax.fori_loop(0, 4, drain, 0)


def shards(features, cotangent, mask, conv_weight, gamma, beta):
    anywhere = pl.BlockSpec(memory_space=pl.ANY)
    vmem = pl.BlockSpec(memory_space=pltpu.VMEM)
    dma = pltpu.SemaphoreType.DMA

    def buf(*shape, dtype=BF16):
        return pltpu.VMEM(shape, dtype)

    panel = (CI, 128)
    dfeatures, dweight, dgains = pl.pallas_call(
        kernel,
        out_shape=(
            buf(1, ROWS, W, C),
            buf(5, 9 * CI, 128, dtype=F32),
            buf(2, C, dtype=F32),
        ),
        in_specs=[anywhere, anywhere, vmem, anywhere, vmem, vmem],
        out_specs=(vmem, vmem, vmem),
        scratch_shapes=[
            buf(ROWS, W, C),
            buf(ROWS, W, C),
            buf(ROWS + 2, W, C),
            buf(ROWS + 2, W, C),
            buf(CELLS + 2 * W, LANES),
            buf(CELLS + 2 * W, HALF),
            buf(C, K9),
            buf(C, CELLS),
            buf(C, CELLS),
            buf(ROWS, W, C, dtype=F32),
            buf(2, 2, 4, *panel, dtype=F32),
            buf(4, 2, 2, *panel, dtype=F32),
            buf(4, 4, *panel, dtype=F32),
            buf(3, 4, 2, 2, 4, *panel),
            buf(3, 2, 2, 4, *panel),
            buf(3, 4, 2, 2, *panel),
            buf(3, 4, 4, *panel),
            buf(2, 2, 4, *panel, dtype=F32),
            buf(4, 2, 2, *panel, dtype=F32),
            buf(4, 4, *panel, dtype=F32),
            buf(2, 2, 4, *panel),
            buf(4, 2, 2, *panel),
            buf(4, 4, *panel),
            buf(3, 2, 2, *panel),
            buf(3, 4, *panel),
            buf(3, 4, *panel),
            buf(2, 2, *panel, dtype=F32),
            buf(4, *panel, dtype=F32),
            buf(4, *panel, dtype=F32),
            buf(3, 3, *panel, dtype=F32),
            buf(2, 2, 4, 3, *panel),
            buf(STRIPS, 2, C, dtype=F32),
            buf(STRIPS, 2, C, dtype=F32),
            buf(2, C, dtype=F32),
            buf(3, 2, C, dtype=F32),
            buf(2, C, dtype=F32),
            buf(2, C, dtype=F32),
            buf(2, C, dtype=F32),
            buf(2, C, dtype=F32),
            dma((2,)),
            dma((9,)),
            dma((7,)),
            dma((7,)),
            dma((7,)),
            dma((7,)),
            dma((2,)),
            dma((2,)),
            dma((1,)),
            dma((1,)),
            dma((ROWS,)),
            dma((ROWS,)),
            dma((2,)),
            dma((2,)),
            dma((3,)),
            dma((3,)),
            dma((4, 3)),
            dma((4, 3)),
            dma((4, 3)),
            dma((4, 3)),
            dma((3, 3)),
            dma((3, 3)),
            dma((3, 3)),
            dma((3, 3)),
            dma((8,)),
            dma((8,)),
            dma((8,)),
            dma((8,)),
            dma((5,)),
            dma((5,)),
        ],
        compiler_params=pltpu.CompilerParams(
            collective_id=0, has_side_effects=True, vmem_limit_bytes=56 * 1024 * 1024
        ),
        cost_estimate=pl.CostEstimate(flops=4 * CELLS * K9 * C, bytes_accessed=13_000_000, transcendentals=CELLS * C),
    )(features, cotangent, mask[0], conv_weight, gamma, beta)
    return dfeatures, jnp.concatenate([dweight[j] for j in range(5)], axis=1), dgains


def solution(mesh):
    placed = (
        P("dp", "tile", None, None),
        P("dp", "tile", None, None),
        P("dp", "tile", None),
        P(),
        P(),
        P(),
    )
    return jax.shard_map(
        shards,
        mesh=mesh,
        in_specs=placed,
        out_specs=(P("dp", "tile", None, None), P("tile", None), P()),
        check_vma=False,
    )
```

```python
import jax
import jax.numpy as jnp
from jax import lax
from jax.experimental import pallas as pl
from jax.experimental.pallas import tpu as pltpu
from jax.sharding import PartitionSpec as P

MESH = pl.DeviceIdType.MESH
BF16 = jnp.bfloat16
F32 = jnp.float32

G = 32
EPSILON = 1e-05
C = 640
PER_GROUP = C // G
ROWS = 8
W = 128
CELLS = ROWS * W
STRIPS = 8
K3 = 3 * C
LANES = 2048
HALF = LANES // 2
BLOCKS = K3 // 128
K9 = 9 * C
CI = C // STRIPS
COUNT = float(ROWS * STRIPS * W * PER_GROUP)
SUB = 256


def kernel(
    x_hbm, cot_hbm, mask_ref, w_hbm, gamma_ref, beta_ref,
    df, dwv, dg_ref,
    x, cot, wpad, wpad_m, cols, cols_m, wmat, act_t, act_m, dn,
    part_sum, own1, own2, s1, r1a, r1b, r1c, t2a, t2b, t2c, h2a, h2b, h2c, r2a, r2b, r2c, t3a, t3b, t3c, r3, gat,
    st, sb, gx, gxr, gz, gzr, gc, gcr,
    load_sem, w_sem,
    st_send, st_recv, sb_send, sb_recv, halo_send, halo_recv,
    wm_send, wm_recv, am_send, am_recv, hm_send, hm_recv,
    a1_send, a1_recv, b1_send, b1_recv, c1_send, c1_recv,
    a2_send, a2_recv, b2_send, b2_recv, c2_send, c2_recv, s3_send, s3_recv,
    gat_send, gat_recv, fwd_send, fwd_recv, g_send, g_recv,
):
    dp = lax.axis_index("dp")
    tile = lax.axis_index("tile")
    core = lax.rem(dp, 2)
    mx = lax.rem(lax.div(dp, 2), 4)
    zlo = lax.div(dp, 8)
    zhi = lax.div(tile, 4)
    my = lax.rem(tile, 4)
    mz = zhi * 2 + zlo
    mate = 1 - core

    def place(px, py, pz, pc):
        return {
            "dp": (lax.rem(pz, 2) * 4 + px) * 2 + pc,
            "tile": lax.div(pz, 2) * 4 + py,
        }

    def x_peer(d):
        return lax.rem(mx + d, 4)

    def y_peer(d):
        return lax.rem(my + d, 4)

    def z_peer(d):
        return lax.rem(mz + d, 4)

    def remote(src, dst, send, recv, device):
        return pltpu.make_async_remote_copy(
            src_ref=src, dst_ref=dst, send_sem=send, recv_sem=recv, device_id=device, device_id_type=MESH
        )

    on_x = [place(x_peer(d), my, mz, core) for d in (1, 2, 3)]
    on_y = [place(mx, y_peer(d), mz, core) for d in (1, 2, 3)]
    on_z = [place(mx, my, z_peer(d), core) for d in (1, 2, 3)]
    on_core = place(mx, my, mz, mate)
    on_zlo = place(mx, my, zhi * 2 + 1 - zlo, core)

    def on_tile(d):
        return {"dp": dp, "tile": lax.rem(tile + d, STRIPS)}

    load_x = pltpu.make_async_copy(x_hbm.at[0], x, load_sem.at[0])
    load_x.start()
    load_cot = pltpu.make_async_copy(cot_hbm.at[0], cot, load_sem.at[1])
    load_cot.start()
    loads_w = [
        pltpu.make_async_copy(w_hbm.at[k // 3, k % 3], wmat.at[:, k * C : (k + 1) * C], w_sem.at[k]) for k in range(9)
    ]

    barrier = pltpu.get_barrier_semaphore()
    for device in on_x + on_y + on_z + [on_core]:
        pl.semaphore_signal(barrier, inc=1, device_id=device, device_id_type=MESH)
    for d in (1, 2, 3):
        other = place(mx, y_peer(d), (1 - zhi) * 2 + zlo, core)
        pl.semaphore_signal(barrier, inc=1, device_id=other, device_id_type=MESH)
        other = place(x_peer(d), my, zhi * 2 + 1 - zlo, core)
        pl.semaphore_signal(barrier, inc=1, device_id=other, device_id_type=MESH)

    load_x.wait()

    def fold(value):
        return jnp.sum(value.reshape(W // 8, 8, C), axis=0)

    zeros8 = jnp.zeros((8, C), F32)
    total = lax.fori_loop(0, ROWS, lambda i, acc: acc + fold(x[i].astype(F32)), zeros8)
    total = jnp.sum(total, axis=0, keepdims=True)
    local_mean = total * (1.0 / CELLS)

    def add_squares(i, acc):
        centered = x[i].astype(F32) - local_mean
        return acc + fold(centered * centered)

    squares = jnp.sum(lax.fori_loop(0, ROWS, add_squares, zeros8), axis=0, keepdims=True)
    st[tile, 0:1] = total
    st[tile, 1:2] = squares
    pl.semaphore_wait(barrier, 16)
    st_copies = [remote(st.at[tile], st.at[tile], st_send.at[d - 1], st_recv.at[d - 1], on_tile(d)) for d in range(1, 8)]
    for copy in st_copies:
        copy.start()

    load_cot.wait()
    for load in loads_w:
        load.start()
    factor = (1.0 + mask_ref[...].astype(F32)).T
    for i in range(ROWS):
        wpad[i + 1] = (cot[i].astype(F32) * factor[:, i : i + 1]).astype(BF16)
    halo = [
        remote(wpad.at[ROWS], wpad.at[0], halo_send.at[0], halo_recv.at[0], on_tile(1)),
        remote(wpad.at[1], wpad.at[ROWS + 1], halo_send.at[1], halo_recv.at[1], on_tile(7)),
    ]
    mate_w = remote(wpad.at[pl.ds(1, ROWS)], wpad_m.at[pl.ds(1, ROWS)], wm_send.at[0], wm_recv.at[0], on_core)
    mate_w.start()
    for copy in halo:
        copy.start()

    rowsw = lax.broadcasted_iota(jnp.int32, (W, C), 0)

    def shifts(value):
        value = value.astype(F32)
        ahead = jnp.where(rowsw == W - 1, 0.0, pltpu.roll(value, W - 1, 0))
        behind = jnp.where(rowsw == 0, 0.0, pltpu.roll(value, 1, 0))
        return ahead.astype(BF16), value.astype(BF16), behind.astype(BF16)

    def spread(r):
        rows = pl.ds(pl.multiple_of(r * W, W), W)
        for ox, shifted in enumerate(shifts(wpad[r])):
            cols[rows, ox * C : (ox + 1) * C] = shifted
        cols[rows, K3:] = jnp.zeros((W, LANES - K3), BF16)

    def spread_mate(r):
        rows = pl.ds(pl.multiple_of(r * W, W), W)
        ahead, middle, behind = shifts(wpad_m[r])
        split = HALF - C

        @pl.when(core == 0)
        def _():
            cols_m[rows, :C] = ahead
            cols_m[rows, C:] = middle[:, :split]

        @pl.when(core == 1)
        def _():
            cols_m[rows, : C - split] = middle[:, split:]
            cols_m[rows, C - split : 2 * C - split] = behind
            cols_m[rows, 2 * C - split :] = jnp.zeros((W, LANES - K3), BF16)

    def inner(step):
        def body(r, carry):
            step(r)
            return carry

        lax.fori_loop(1, ROWS + 1, body, 0)

    inner(spread)

    for copy in st_copies:
        copy.wait_recv()
    chan = lax.broadcasted_iota(jnp.int32, (C, 128), 0).astype(F32)
    group = lax.broadcasted_iota(jnp.int32, (C, 128), 1).astype(F32)
    member = jnp.where(jnp.floor((chan + 0.5) * (1.0 / PER_GROUP)) == group, 1.0, 0.0)
    chan_t = lax.broadcasted_iota(jnp.int32, (128, C), 1).astype(F32)
    group_t = lax.broadcasted_iota(jnp.int32, (128, C), 0).astype(F32)
    member_t = jnp.where(jnp.floor((chan_t + 0.5) * (1.0 / PER_GROUP)) == group_t, 1.0, 0.0)

    def to_groups(value):
        return jnp.dot(value, member, precision=lax.Precision.HIGHEST, preferred_element_type=F32)

    def to_channels(value):
        return jnp.dot(value, member_t, precision=lax.Precision.HIGHEST, preferred_element_type=F32)

    sums = st[0]
    for i in range(1, STRIPS):
        sums = sums + st[i]
    mean = to_channels(to_groups(jnp.broadcast_to(sums[0:1], (8, C))) * (1.0 / COUNT))[0:1]
    apart = jnp.zeros((1, C), F32)
    for i in range(STRIPS):
        centered = st[i, 0:1] * (1.0 / CELLS) - mean
        apart = apart + centered * centered
    spread_sq = apart * float(CELLS) + sums[1:2]
    variance = to_groups(jnp.broadcast_to(spread_sq, (8, C))) * (1.0 / COUNT)
    inverse = to_channels(lax.rsqrt(variance + EPSILON))[0:1]
    gamma = gamma_ref[...].reshape(1, C)
    beta = beta_ref[...].reshape(1, C)

    def mate_act(i):
        block = pl.ds(pl.multiple_of(i * W, W), W)
        return remote(act_t.at[:, block], act_m.at[:, block], am_send.at[i], am_recv.at[i], on_core)

    def activate(i, carry):
        scaled = (x[i].astype(F32) - mean) * inverse
        normed = scaled * gamma + beta
        sig = 0.5 + 0.5 * jnp.tanh(0.5 * normed)
        act = normed * sig
        dn[i] = sig * (1.0 + normed * (1.0 - sig))
        act_t[:, pl.ds(pl.multiple_of(i * W, W), W)] = act.T.astype(BF16)
        mate_act(i).start()
        return carry

    lax.fori_loop(0, ROWS, activate, 0)

    for copy in halo:
        copy.wait_recv()

    @pl.when(tile == 0)
    def _():
        wpad[0] = jnp.zeros((W, C), BF16)

    @pl.when(tile == STRIPS - 1)
    def _():
        wpad[ROWS + 1] = jnp.zeros((W, C), BF16)

    mate_edge = [
        remote(wpad.at[r], wpad_m.at[r], hm_send.at[n], hm_recv.at[n], on_core) for n, r in enumerate((0, ROWS + 1))
    ]
    for copy in mate_edge:
        copy.start()
    spread(0)
    spread(ROWS + 1)
    mate_w.wait_recv()
    inner(spread_mate)
    for copy in mate_edge:
        copy.wait_recv()
    spread_mate(0)
    spread_mate(ROWS + 1)
    for i in range(ROWS):
        mate_act(i).wait_recv()

    def partial(part, xq):
        rows = pl.ds((2 - part) * W, CELLS)
        own = cols[rows, pl.ds(pl.multiple_of(core * HALF + xq * 256, 256), 256)]
        theirs = cols_m[rows, pl.ds(pl.multiple_of(xq * 256, 256), 256)]
        return jnp.dot(act_t[...], own, preferred_element_type=F32) + jnp.dot(
            act_m[...], theirs, preferred_element_type=F32
        )

    def turn(s):
        return jnp.where(s == 0, 1, jnp.where(s == 1, 3, jnp.where(s == 2, 2, 0)))

    def x_copy(s):
        xq = x_peer(turn(s))
        return remote(s1.at[0, xq], r1a.at[s], a1_send.at[s], a1_recv.at[s], place(xq, my, mz, core))

    def y_copy(s, d):
        xq = x_peer(turn(s))
        src = s1.at[1, xq, :, :, y_peer(d)]
        return remote(src, r1b.at[d - 1, xq], b1_send.at[s, d - 1], b1_recv.at[s, d - 1], on_y[d - 1])

    def z_copy(s, d):
        xq = x_peer(turn(s))
        src = s1.at[2, xq, lax.rem(z_peer(d), 2), lax.div(z_peer(d), 2)]
        return remote(src, r1c.at[d - 1, xq], c1_send.at[s, d - 1], c1_recv.at[s, d - 1], on_z[d - 1])

    def grad_step(s, carry):
        xq = x_peer(turn(s))
        for part in range(3):
            result = partial(part, xq)
            for b in range(2):
                piece = result[:, b * 128 : (b + 1) * 128].reshape(2, 4, CI, 128)
                part_sum[b] = piece
                s1[part, xq, b] = piece.astype(BF16)
            if part == 0:

                @pl.when(s < 3)
                def _():
                    x_copy(s).start()

            for d in (1, 3, 2):
                if part == 1:
                    y_copy(s, d).start()
                if part == 2:
                    z_copy(s, d).start()
            if part == 1:
                own1[xq] = part_sum[:, :, my]
            if part == 2:
                own2[xq] = part_sum[zlo, zhi]
            if part == 0:

                @pl.when(s == 3)
                def _():
                    t2a[...] = part_sum[...]
        return carry

    lax.fori_loop(0, 4, grad_step, 0)

    for load in loads_w:
        load.wait()

    def dactive_step(i, carry):
        s0, s1_ = carry
        dact = jnp.zeros((SUB, C), F32)
        for oy in range(3):
            window = cols[pl.ds(pl.multiple_of(i * SUB + (2 - oy) * W, W), SUB), :K3]
            dact = dact + lax.dot_general(
                window, wmat[:, oy * K3 : (oy + 1) * K3], (((1,), (1,)), ((), ())), preferred_element_type=F32
            )
        for j in range(SUB // W):
            r = i * (SUB // W) + j
            dnormed = dact[j * W : (j + 1) * W] * dn[r]
            dn[r] = dnormed
            scaled = (x[r].astype(F32) - mean) * inverse
            s0 = s0 + fold(dnormed)
            s1_ = s1_ + fold(dnormed * scaled)
        return s0, s1_

    def z_of(d):
        return lax.rem(z_peer(d), 2), lax.div(z_peer(d), 2)

    def b2_copy(i, d):
        xq = x_peer(turn(i))
        zq, zh = z_of(d)
        return remote(h2b.at[xq, zq, zh], r2b.at[d - 1, xq], b2_send.at[i, d - 1], b2_recv.at[i, d - 1], on_z[d - 1])

    def c2_copy(i):
        xq = x_peer(turn(i))
        return remote(h2c.at[xq], r2c.at[i], c2_send.at[i], c2_recv.at[i], place(xq, my, mz, core))

    def a2_copy(n, d):
        zq, zh = z_of(n)
        return remote(h2a.at[zq, zh, y_peer(d)], r2a.at[d - 1, n], a2_send.at[n, d - 1], a2_recv.at[n, d - 1], on_y[d - 1])

    def a3_copy(d):
        zq, zh = z_of(d)
        return remote(t3a.at[zq, zh], r3.at[0, d - 1], s3_send.at[0, d - 1], s3_recv.at[0, d - 1], on_z[d - 1])

    def b3_copy(d):
        return remote(t3b.at[x_peer(d)], r3.at[1, d - 1], s3_send.at[1, d - 1], s3_recv.at[1, d - 1], on_x[d - 1])

    def c3_copy(d):
        return remote(t3c.at[y_peer(d)], r3.at[2, d - 1], s3_send.at[2, d - 1], s3_recv.at[2, d - 1], on_y[d - 1])

    def first_bc(i):
        xq = x_peer(turn(i))
        for d in (1, 2, 3):
            y_copy(i, d).wait_recv()
        total = own1[xq] + r1b[0, xq].astype(F32) + r1b[1, xq].astype(F32) + r1b[2, xq].astype(F32)
        t2b[xq] = total
        h2b[xq] = total.astype(BF16)
        for d in (1, 3, 2):
            b2_copy(i, d).start()
        for d in (1, 2, 3):
            z_copy(i, d).wait_recv()
        total = own2[xq] + r1c[0, xq].astype(F32) + r1c[1, xq].astype(F32) + r1c[2, xq].astype(F32)
        t2c[xq] = total
        h2c[xq] = total.astype(BF16)
        if i < 3:
            c2_copy(i).start()

    def first_a():
        for i in range(3):
            x_copy(i).wait_recv()
        total = t2a[...] + r1a[0].astype(F32) + r1a[1].astype(F32) + r1a[2].astype(F32)
        t2a[...] = total
        h2a[...] = total.astype(BF16)
        for n in (1, 3, 2, 0):
            for d in (1, 3, 2):
                a2_copy(n, d).start()

    sums01 = (zeros8, zeros8)
    sums01 = dactive_step(0, sums01)
    first_bc(0)
    sums01 = dactive_step(1, sums01)
    first_bc(1)
    first_bc(2)
    first_a()
    first_bc(3)
    sums01 = dactive_step(2, sums01)
    sums01 = dactive_step(3, sums01)
    sum0 = jnp.sum(sums01[0], axis=0, keepdims=True)
    sum1 = jnp.sum(sums01[1], axis=0, keepdims=True)
    sb[tile, 0:1] = sum1
    sb[tile, 1:2] = sum0
    sb_copies = [remote(sb.at[tile], sb.at[tile], sb_send.at[d - 1], sb_recv.at[d - 1], on_tile(d)) for d in range(1, 8)]
    for copy in sb_copies:
        copy.start()

    for i, n in ((0, 1), (1, 3), (2, 2), (3, 0)):
        xq = x_peer(n)
        for d in (1, 2, 3):
            b2_copy(i, d).wait_recv()
        t3b[xq] = (
            t2b[xq, zlo, zhi] + r2b[0, xq].astype(F32) + r2b[1, xq].astype(F32) + r2b[2, xq].astype(F32)
        )
        if n:
            b3_copy(n).start()
        zq, zh = z_of(n)
        for d in (1, 2, 3):
            a2_copy(n, d).wait_recv()
        t3a[zq, zh] = (
            t2a[zq, zh, my] + r2a[0, n].astype(F32) + r2a[1, n].astype(F32) + r2a[2, n].astype(F32)
        )
        if n:
            a3_copy(n).start()
    for i in range(3):
        c2_copy(i).wait_recv()
    t3c[...] = t2c[mx] + r2c[0].astype(F32) + r2c[1].astype(F32) + r2c[2].astype(F32)
    for d in (1, 3, 2):
        c3_copy(d).start()

    for copy in sb_copies:
        copy.wait_recv()
    gsum = sb[0]
    for i in range(1, STRIPS):
        gsum = gsum + sb[i]
    gx[...] = gsum
    g1 = [remote(gx, gxr.at[d - 1], g_send.at[d - 1], g_recv.at[d - 1], on_x[d - 1]) for d in (1, 2, 3)]
    for copy in g1:
        copy.start()

    order = ((0, 1), (0, 3), (1, 0), (0, 2), (1, 1), (1, 3), (1, 2))

    def gat_copy(part, dz, dx):
        mine = gat.at[core, zlo, mx, part]
        target = place(x_peer(dx), my, zhi * 2 + lax.rem(zlo + dz, 2), core)
        return remote(mine, mine, gat_send.at[part, dz * 4 + dx], gat_recv.at[part, dz * 4 + dx], target)

    def mate_gat(part, dz, dx):
        block = gat.at[core, lax.rem(zlo + dz, 2), lax.rem(mx + 4 - dx, 4), part]
        return remote(block, block, fwd_send.at[part, dz * 4 + dx], fwd_recv.at[part, dz * 4 + dx], on_core)

    def assemble(c, part, dz, dx):
        zq = lax.rem(zlo + dz, 2)
        xq = lax.rem(mx + 4 - dx, 4)
        b = c * 8 + xq * 2 + zq

        @pl.when(b < BLOCKS)
        def _():
            k = part * 3 + lax.div(b, 5)
            j = lax.rem(b, 5)
            dwv[j, pl.ds(k, CI, stride=9), :] = gat[c, zq, xq, part].astype(F32)

    for part, third in ((1, b3_copy), (0, a3_copy), (2, c3_copy)):
        for d in (1, 2, 3):
            third(d).wait_recv()
        own = (t3a[zlo, zhi], t3b[mx], t3c[my])[part]
        gat[core, zlo, mx, part] = (own + r3[part, 0] + r3[part, 1] + r3[part, 2]).astype(BF16)
        for dz, dx in order:
            gat_copy(part, dz, dx).start()
        mate_gat(part, 0, 0).start()

    weighed = gsum * gamma
    row8 = lax.broadcasted_iota(jnp.int32, (8, C), 0)
    weighed = jnp.where(row8 == 0, weighed[0:1], weighed[1:2])
    moments = to_channels(to_groups(weighed) * (1.0 / COUNT))
    second = moments[0:1]
    first = moments[1:2]

    for copy in g1:
        copy.wait_recv()
    gz[...] = gx[...] + gxr[0] + gxr[1] + gxr[2]
    g2 = remote(gz, gzr, g_send.at[3], g_recv.at[3], on_zlo)
    g2.start()

    def finish(i, carry):
        scaled = (x[i].astype(F32) - mean) * inverse
        grad = inverse * (dn[i] * gamma - first - scaled * second) + wpad[i + 1].astype(F32)
        df[0, i] = grad.astype(BF16)
        return carry

    lax.fori_loop(0, ROWS, finish, 0)
    g2.wait_recv()
    gc[...] = gz[...] + gzr[...]
    g3 = remote(gc, gcr, g_send.at[4], g_recv.at[4], on_core)
    g3.start()

    for part in (1, 0, 2):
        assemble(core, part, 0, 0)
    for dz, dx in order:
        for part in (1, 0, 2):
            gat_copy(part, dz, dx).wait_recv()
            mate_gat(part, dz, dx).start()
            assemble(core, part, dz, dx)
    g3.wait_recv()
    dg_ref[...] = gc[...] + gcr[...]
    for dz, dx in ((0, 0),) + order:
        for part in (1, 0, 2):
            mate_gat(part, dz, dx).wait_recv()
            assemble(mate, part, dz, dx)

    for copy in st_copies + halo + [mate_w] + mate_edge + sb_copies + g1 + [g2, g3]:
        copy.wait_send()
    for part in range(3):
        mate_gat(part, 0, 0).wait_send()
        for dz, dx in order:
            gat_copy(part, dz, dx).wait_send()
            mate_gat(part, dz, dx).wait_send()
    for d in (1, 2, 3):
        a3_copy(d).wait_send()
        b3_copy(d).wait_send()
        c3_copy(d).wait_send()

    def drain(s, carry):
        mate_act(s * 2).wait_send()
        mate_act(s * 2 + 1).wait_send()
        for d in (1, 2, 3):
            y_copy(s, d).wait_send()
            z_copy(s, d).wait_send()
            a2_copy(s, d).wait_send()
            b2_copy(s, d).wait_send()

        @pl.when(s < 3)
        def _():
            x_copy(s).wait_send()
            c2_copy(s).wait_send()

        return carry

    lax.fori_loop(0, 4, drain, 0)


def shards(features, cotangent, mask, conv_weight, gamma, beta):
    anywhere = pl.BlockSpec(memory_space=pl.ANY)
    vmem = pl.BlockSpec(memory_space=pltpu.VMEM)
    dma = pltpu.SemaphoreType.DMA

    def buf(*shape, dtype=BF16):
        return pltpu.VMEM(shape, dtype)

    panel = (CI, 128)
    dfeatures, dweight, dgains = pl.pallas_call(
        kernel,
        out_shape=(
            buf(1, ROWS, W, C),
            buf(5, 9 * CI, 128, dtype=F32),
            buf(2, C, dtype=F32),
        ),
        in_specs=[anywhere, anywhere, vmem, anywhere, vmem, vmem],
        out_specs=(vmem, vmem, vmem),
        scratch_shapes=[
            buf(ROWS, W, C),
            buf(ROWS, W, C),
            buf(ROWS + 2, W, C),
            buf(ROWS + 2, W, C),
            buf(CELLS + 2 * W, LANES),
            buf(CELLS + 2 * W, HALF),
            buf(C, K9),
            buf(C, CELLS),
            buf(C, CELLS),
            buf(ROWS, W, C, dtype=F32),
            buf(2, 2, 4, *panel, dtype=F32),
            buf(4, 2, 2, *panel, dtype=F32),
            buf(4, 4, *panel, dtype=F32),
            buf(3, 4, 2, 2, 4, *panel),
            buf(3, 2, 2, 4, *panel),
            buf(3, 4, 2, 2, *panel),
            buf(3, 4, 4, *panel),
            buf(2, 2, 4, *panel, dtype=F32),
            buf(4, 2, 2, *panel, dtype=F32),
            buf(4, 4, *panel, dtype=F32),
            buf(2, 2, 4, *panel),
            buf(4, 2, 2, *panel),
            buf(4, 4, *panel),
            buf(3, 4, *panel),
            buf(3, 4, *panel),
            buf(3, 4, *panel),
            buf(2, 2, *panel, dtype=F32),
            buf(4, *panel, dtype=F32),
            buf(4, *panel, dtype=F32),
            buf(3, 3, *panel, dtype=F32),
            buf(2, 2, 4, 3, *panel),
            buf(STRIPS, 2, C, dtype=F32),
            buf(STRIPS, 2, C, dtype=F32),
            buf(2, C, dtype=F32),
            buf(3, 2, C, dtype=F32),
            buf(2, C, dtype=F32),
            buf(2, C, dtype=F32),
            buf(2, C, dtype=F32),
            buf(2, C, dtype=F32),
            dma((2,)),
            dma((9,)),
            dma((7,)),
            dma((7,)),
            dma((7,)),
            dma((7,)),
            dma((2,)),
            dma((2,)),
            dma((1,)),
            dma((1,)),
            dma((ROWS,)),
            dma((ROWS,)),
            dma((2,)),
            dma((2,)),
            dma((3,)),
            dma((3,)),
            dma((4, 3)),
            dma((4, 3)),
            dma((4, 3)),
            dma((4, 3)),
            dma((4, 3)),
            dma((4, 3)),
            dma((4, 3)),
            dma((4, 3)),
            dma((3,)),
            dma((3,)),
            dma((3, 3)),
            dma((3, 3)),
            dma((3, 8)),
            dma((3, 8)),
            dma((3, 8)),
            dma((3, 8)),
            dma((5,)),
            dma((5,)),
        ],
        compiler_params=pltpu.CompilerParams(
            collective_id=0, has_side_effects=True, vmem_limit_bytes=56 * 1024 * 1024
        ),
        cost_estimate=pl.CostEstimate(flops=4 * CELLS * K9 * C, bytes_accessed=13_000_000, transcendentals=CELLS * C),
    )(features, cotangent, mask[0], conv_weight, gamma, beta)
    return dfeatures, jnp.concatenate([dweight[j] for j in range(5)], axis=1), dgains


def solution(mesh):
    placed = (
        P("dp", "tile", None, None),
        P("dp", "tile", None, None),
        P("dp", "tile", None),
        P(),
        P(),
        P(),
    )
    return jax.shard_map(
        shards,
        mesh=mesh,
        in_specs=placed,
        out_specs=(P("dp", "tile", None, None), P("tile", None), P()),
        check_vma=False,
    )
```

```python
import jax
import jax.numpy as jnp
from jax import lax
from jax.experimental import pallas as pl
from jax.experimental.pallas import tpu as pltpu
from jax.sharding import PartitionSpec as P

MESH = pl.DeviceIdType.MESH
BF16 = jnp.bfloat16
F32 = jnp.float32

G = 32
EPSILON = 1e-05
C = 640
PER_GROUP = C // G
ROWS = 8
W = 128
CELLS = ROWS * W
STRIPS = 8
K3 = 3 * C
LANES = 2048
HALF = LANES // 2
BLOCKS = K3 // 128
K9 = 9 * C
CI = C // STRIPS
COUNT = float(ROWS * STRIPS * W * PER_GROUP)
SUB = 512


def kernel(
    x_hbm, cot_hbm, mask_hbm, w_hbm, gamma_hbm, beta_hbm,
    df, dwv, dg_ref,
    mask_ref, gamma_ref, beta_ref, x, cot, wpad, wpad_m, cols, cols_m, wmat, act_t, act_m, dn,
    part_sum, own1, own2, s1, r1a, r1b, r1c, t2a, t2b, t2c, h2a, h2b, h2c, r2a, r2b, r2c, t3a, t3b, t3c, r3, gat,
    st, sb, gx, gxr, gz, gzr, gc, gcr,
    load_sem, w_sem,
    st_send, st_recv, sb_send, sb_recv, halo_send, halo_recv,
    wm_send, wm_recv, am_send, am_recv, hm_send, hm_recv,
    a1_send, a1_recv, b1_send, b1_recv, c1_send, c1_recv,
    a2_send, a2_recv, b2_send, b2_recv, c2_send, c2_recv, s3_send, s3_recv,
    gat_send, gat_recv, fwd_send, fwd_recv, g_send, g_recv,
):
    dp = lax.axis_index("dp")
    tile = lax.axis_index("tile")
    core = lax.rem(dp, 2)
    mx = lax.rem(lax.div(dp, 2), 4)
    zlo = lax.div(dp, 8)
    zhi = lax.div(tile, 4)
    my = lax.rem(tile, 4)
    mz = zhi * 2 + zlo
    mate = 1 - core

    def place(px, py, pz, pc):
        return {
            "dp": (lax.rem(pz, 2) * 4 + px) * 2 + pc,
            "tile": lax.div(pz, 2) * 4 + py,
        }

    def x_peer(d):
        return lax.rem(mx + d, 4)

    def y_peer(d):
        return lax.rem(my + d, 4)

    def z_peer(d):
        return lax.rem(mz + d, 4)

    def remote(src, dst, send, recv, device):
        return pltpu.make_async_remote_copy(
            src_ref=src, dst_ref=dst, send_sem=send, recv_sem=recv, device_id=device, device_id_type=MESH
        )

    on_x = [place(x_peer(d), my, mz, core) for d in (1, 2, 3)]
    on_y = [place(mx, y_peer(d), mz, core) for d in (1, 2, 3)]
    on_z = [place(mx, my, z_peer(d), core) for d in (1, 2, 3)]
    on_core = place(mx, my, mz, mate)
    on_zlo = place(mx, my, zhi * 2 + 1 - zlo, core)

    def on_tile(d):
        return {"dp": dp, "tile": lax.rem(tile + d, STRIPS)}

    load_x = pltpu.make_async_copy(x_hbm.at[0], x, load_sem.at[0])
    load_x.start()
    load_cot = pltpu.make_async_copy(cot_hbm.at[0], cot, load_sem.at[1])
    load_cot.start()
    load_mask = pltpu.make_async_copy(mask_hbm.at[0], mask_ref, load_sem.at[2])
    load_gamma = pltpu.make_async_copy(gamma_hbm, gamma_ref, load_sem.at[3])
    load_beta = pltpu.make_async_copy(beta_hbm, beta_ref, load_sem.at[4])
    for load in (load_mask, load_gamma, load_beta):
        load.start()
    loads_w = [
        pltpu.make_async_copy(w_hbm.at[k // 3, k % 3], wmat.at[:, k * C : (k + 1) * C], w_sem.at[k]) for k in range(9)
    ]

    barrier = pltpu.get_barrier_semaphore()
    for device in on_x + on_y + on_z + [on_core]:
        pl.semaphore_signal(barrier, inc=1, device_id=device, device_id_type=MESH)
    for d in (1, 2, 3):
        other = place(mx, y_peer(d), (1 - zhi) * 2 + zlo, core)
        pl.semaphore_signal(barrier, inc=1, device_id=other, device_id_type=MESH)
        other = place(x_peer(d), my, zhi * 2 + 1 - zlo, core)
        pl.semaphore_signal(barrier, inc=1, device_id=other, device_id_type=MESH)

    load_x.wait()

    def fold(value):
        return jnp.sum(value.reshape(W // 8, 8, C), axis=0)

    zeros8 = jnp.zeros((8, C), F32)
    total = lax.fori_loop(0, ROWS, lambda i, acc: acc + fold(x[i].astype(F32)), zeros8)
    total = jnp.sum(total, axis=0, keepdims=True)
    local_mean = total * (1.0 / CELLS)

    def add_squares(i, acc):
        centered = x[i].astype(F32) - local_mean
        return acc + fold(centered * centered)

    squares = jnp.sum(lax.fori_loop(0, ROWS, add_squares, zeros8), axis=0, keepdims=True)
    st[tile, 0:1] = total
    st[tile, 1:2] = squares
    pl.semaphore_wait(barrier, 16)
    st_copies = [remote(st.at[tile], st.at[tile], st_send.at[d - 1], st_recv.at[d - 1], on_tile(d)) for d in range(1, 8)]
    for copy in st_copies:
        copy.start()

    load_cot.wait()
    for load in (load_mask, load_gamma, load_beta):
        load.wait()
    for load in loads_w:
        load.start()
    factor = (1.0 + mask_ref[...].astype(F32)).T
    for i in range(ROWS):
        wpad[i + 1] = (cot[i].astype(F32) * factor[:, i : i + 1]).astype(BF16)
    halo = [
        remote(wpad.at[ROWS], wpad.at[0], halo_send.at[0], halo_recv.at[0], on_tile(1)),
        remote(wpad.at[1], wpad.at[ROWS + 1], halo_send.at[1], halo_recv.at[1], on_tile(7)),
    ]
    mate_w = remote(wpad.at[pl.ds(1, ROWS)], wpad_m.at[pl.ds(1, ROWS)], wm_send.at[0], wm_recv.at[0], on_core)
    mate_w.start()
    for copy in halo:
        copy.start()

    rowsw = lax.broadcasted_iota(jnp.int32, (W, C), 0)

    def shifts(value):
        value = value.astype(F32)
        ahead = jnp.where(rowsw == W - 1, 0.0, pltpu.roll(value, W - 1, 0))
        behind = jnp.where(rowsw == 0, 0.0, pltpu.roll(value, 1, 0))
        return ahead.astype(BF16), value.astype(BF16), behind.astype(BF16)

    def spread(r):
        rows = pl.ds(pl.multiple_of(r * W, W), W)
        for ox, shifted in enumerate(shifts(wpad[r])):
            cols[rows, ox * C : (ox + 1) * C] = shifted
        cols[rows, K3:] = jnp.zeros((W, LANES - K3), BF16)

    def spread_mate(r):
        rows = pl.ds(pl.multiple_of(r * W, W), W)
        ahead, middle, behind = shifts(wpad_m[r])
        split = HALF - C

        @pl.when(core == 0)
        def _():
            cols_m[rows, :C] = ahead
            cols_m[rows, C:] = middle[:, :split]

        @pl.when(core == 1)
        def _():
            cols_m[rows, : C - split] = middle[:, split:]
            cols_m[rows, C - split : 2 * C - split] = behind
            cols_m[rows, 2 * C - split :] = jnp.zeros((W, LANES - K3), BF16)

    def inner(step):
        def body(r, carry):
            step(r)
            return carry

        lax.fori_loop(1, ROWS + 1, body, 0)

    inner(spread)

    chan = lax.broadcasted_iota(jnp.int32, (C, 128), 0).astype(F32)
    group = lax.broadcasted_iota(jnp.int32, (C, 128), 1).astype(F32)
    member = jnp.where(jnp.floor((chan + 0.5) * (1.0 / PER_GROUP)) == group, 1.0, 0.0).astype(BF16)
    chan_t = lax.broadcasted_iota(jnp.int32, (128, C), 1).astype(F32)
    group_t = lax.broadcasted_iota(jnp.int32, (128, C), 0).astype(F32)
    member_t = jnp.where(jnp.floor((chan_t + 0.5) * (1.0 / PER_GROUP)) == group_t, 1.0, 0.0).astype(BF16)

    def in_parts(value):
        high = value.astype(BF16).astype(F32)
        middle = (value - high).astype(BF16).astype(F32)
        return jnp.concatenate([high, middle, value - high - middle], axis=0).astype(BF16)

    def times(value, table):
        product = jnp.dot(in_parts(value), table, preferred_element_type=F32)
        return product[0:8] + product[8:16] + product[16:24]

    def to_groups(value):
        return times(value, member)

    def to_channels(value):
        return times(value, member_t)

    for copy in st_copies:
        copy.wait_recv()
    sums = st[0]
    for i in range(1, STRIPS):
        sums = sums + st[i]
    mean = to_channels(to_groups(jnp.broadcast_to(sums[0:1], (8, C))) * (1.0 / COUNT))[0:1]
    apart = jnp.zeros((1, C), F32)
    for i in range(STRIPS):
        centered = st[i, 0:1] * (1.0 / CELLS) - mean
        apart = apart + centered * centered
    spread_sq = apart * float(CELLS) + sums[1:2]
    variance = to_groups(jnp.broadcast_to(spread_sq, (8, C))) * (1.0 / COUNT)
    inverse = to_channels(lax.rsqrt(variance + EPSILON))[0:1]
    gamma = gamma_ref[...].reshape(1, C)
    beta = beta_ref[...].reshape(1, C)

    def mate_act(i):
        block = pl.ds(pl.multiple_of(i * W, W), W)
        return remote(act_t.at[:, block], act_m.at[:, block], am_send.at[i], am_recv.at[i], on_core)

    def activate(i, carry):
        scaled = (x[i].astype(F32) - mean) * inverse
        normed = scaled * gamma + beta
        sig = 0.5 + 0.5 * jnp.tanh(0.5 * normed)
        act = normed * sig
        dn[i] = sig * (1.0 + normed * (1.0 - sig))
        act_t[:, pl.ds(pl.multiple_of(i * W, W), W)] = act.T.astype(BF16)
        mate_act(i).start()
        return carry

    lax.fori_loop(0, ROWS, activate, 0)

    for copy in halo:
        copy.wait_recv()

    @pl.when(tile == 0)
    def _():
        wpad[0] = jnp.zeros((W, C), BF16)

    @pl.when(tile == STRIPS - 1)
    def _():
        wpad[ROWS + 1] = jnp.zeros((W, C), BF16)

    mate_edge = [
        remote(wpad.at[r], wpad_m.at[r], hm_send.at[n], hm_recv.at[n], on_core) for n, r in enumerate((0, ROWS + 1))
    ]
    for copy in mate_edge:
        copy.start()
    spread(0)
    spread(ROWS + 1)
    mate_w.wait_recv()
    inner(spread_mate)
    for copy in mate_edge:
        copy.wait_recv()
    spread_mate(0)
    spread_mate(ROWS + 1)
    for i in range(ROWS):
        mate_act(i).wait_recv()

    def partial(part, xq):
        rows = pl.ds((2 - part) * W, CELLS)
        own = cols[rows, pl.ds(pl.multiple_of(core * HALF + xq * 256, 256), 256)]
        theirs = cols_m[rows, pl.ds(pl.multiple_of(xq * 256, 256), 256)]
        return jnp.dot(act_t[...], own, preferred_element_type=F32) + jnp.dot(
            act_m[...], theirs, preferred_element_type=F32
        )

    def turn(s):
        return jnp.where(s == 0, 2, jnp.where(s == 1, 1, jnp.where(s == 2, 3, 0)))

    def x_copy(s):
        xq = x_peer(turn(s))
        return remote(s1.at[0, xq], r1a.at[s], a1_send.at[s], a1_recv.at[s], place(xq, my, mz, core))

    def y_copy(s, d):
        xq = x_peer(turn(s))
        src = s1.at[1, xq, :, :, y_peer(d)]
        return remote(src, r1b.at[d - 1, xq], b1_send.at[s, d - 1], b1_recv.at[s, d - 1], on_y[d - 1])

    def z_copy(s, d):
        xq = x_peer(turn(s))
        src = s1.at[2, xq, lax.rem(z_peer(d), 2), lax.div(z_peer(d), 2)]
        return remote(src, r1c.at[d - 1, xq], c1_send.at[s, d - 1], c1_recv.at[s, d - 1], on_z[d - 1])

    def grad_step(s, carry):
        xq = x_peer(turn(s))
        for part in range(3):
            result = partial(part, xq)
            for b in range(2):
                piece = result[:, b * 128 : (b + 1) * 128].reshape(2, 4, CI, 128)
                part_sum[b] = piece
                s1[part, xq, b] = piece.astype(BF16)
            if part == 0:

                @pl.when(s < 3)
                def _():
                    x_copy(s).start()

            for d in (1, 3, 2):
                if part == 1:
                    y_copy(s, d).start()
                if part == 2:
                    z_copy(s, d).start()
            if part == 1:
                own1[xq] = part_sum[:, :, my]
            if part == 2:
                own2[xq] = part_sum[zlo, zhi]
            if part == 0:

                @pl.when(s == 3)
                def _():
                    t2a[...] = part_sum[...]
        return carry

    lax.fori_loop(0, 4, grad_step, 0)

    for load in loads_w:
        load.wait()

    def dactive_step(i, carry):
        s0, s1_ = carry
        dact = jnp.zeros((SUB, C), F32)
        for oy in range(3):
            window = cols[pl.ds(pl.multiple_of(i * SUB + (2 - oy) * W, W), SUB), :K3]
            dact = dact + lax.dot_general(
                window, wmat[:, oy * K3 : (oy + 1) * K3], (((1,), (1,)), ((), ())), preferred_element_type=F32
            )
        for j in range(SUB // W):
            r = i * (SUB // W) + j
            dnormed = dact[j * W : (j + 1) * W] * dn[r]
            dn[r] = dnormed
            scaled = (x[r].astype(F32) - mean) * inverse
            s0 = s0 + fold(dnormed)
            s1_ = s1_ + fold(dnormed * scaled)
        return s0, s1_

    def z_of(d):
        return lax.rem(z_peer(d), 2), lax.div(z_peer(d), 2)

    def b2_copy(i, d):
        xq = x_peer(turn(i))
        zq, zh = z_of(d)
        return remote(h2b.at[xq, zq, zh], r2b.at[d - 1, xq], b2_send.at[i, d - 1], b2_recv.at[i, d - 1], on_z[d - 1])

    def c2_copy(i):
        xq = x_peer(turn(i))
        return remote(h2c.at[xq], r2c.at[i], c2_send.at[i], c2_recv.at[i], place(xq, my, mz, core))

    def a2_copy(n, d):
        zq, zh = z_of(n)
        return remote(h2a.at[zq, zh, y_peer(d)], r2a.at[d - 1, n], a2_send.at[n, d - 1], a2_recv.at[n, d - 1], on_y[d - 1])

    def a3_copy(d):
        zq, zh = z_of(d)
        return remote(t3a.at[zq, zh], r3.at[0, d - 1], s3_send.at[0, d - 1], s3_recv.at[0, d - 1], on_z[d - 1])

    def b3_copy(d):
        return remote(t3b.at[x_peer(d)], r3.at[1, d - 1], s3_send.at[1, d - 1], s3_recv.at[1, d - 1], on_x[d - 1])

    def c3_copy(d):
        return remote(t3c.at[y_peer(d)], r3.at[2, d - 1], s3_send.at[2, d - 1], s3_recv.at[2, d - 1], on_y[d - 1])

    def first_bc(i):
        xq = x_peer(turn(i))
        for d in (1, 2, 3):
            y_copy(i, d).wait_recv()
        total = own1[xq] + r1b[0, xq].astype(F32) + r1b[1, xq].astype(F32) + r1b[2, xq].astype(F32)
        t2b[xq] = total
        h2b[xq] = total.astype(BF16)
        for d in (1, 3, 2):
            b2_copy(i, d).start()
        for d in (1, 2, 3):
            z_copy(i, d).wait_recv()
        total = own2[xq] + r1c[0, xq].astype(F32) + r1c[1, xq].astype(F32) + r1c[2, xq].astype(F32)
        t2c[xq] = total
        h2c[xq] = total.astype(BF16)
        if i < 3:
            c2_copy(i).start()

    def first_a():
        for i in range(3):
            x_copy(i).wait_recv()
        total = t2a[...] + r1a[0].astype(F32) + r1a[1].astype(F32) + r1a[2].astype(F32)
        t2a[...] = total
        h2a[...] = total.astype(BF16)
        for n in (1, 3, 2, 0):
            for d in (1, 3, 2):
                a2_copy(n, d).start()

    sums01 = (zeros8, zeros8)
    sums01 = dactive_step(0, sums01)
    first_bc(0)
    first_bc(1)
    first_bc(2)
    first_a()
    first_bc(3)
    sums01 = dactive_step(1, sums01)
    sum0 = jnp.sum(sums01[0], axis=0, keepdims=True)
    sum1 = jnp.sum(sums01[1], axis=0, keepdims=True)
    sb[tile, 0:1] = sum1
    sb[tile, 1:2] = sum0
    sb_copies = [remote(sb.at[tile], sb.at[tile], sb_send.at[d - 1], sb_recv.at[d - 1], on_tile(d)) for d in range(1, 8)]
    for copy in sb_copies:
        copy.start()

    for i, n in ((0, 2), (1, 1), (2, 3), (3, 0)):
        xq = x_peer(n)
        for d in (1, 2, 3):
            b2_copy(i, d).wait_recv()
        t3b[xq] = (
            t2b[xq, zlo, zhi] + r2b[0, xq].astype(F32) + r2b[1, xq].astype(F32) + r2b[2, xq].astype(F32)
        )
        if n:
            b3_copy(n).start()
        zq, zh = z_of(n)
        for d in (1, 2, 3):
            a2_copy(n, d).wait_recv()
        t3a[zq, zh] = (
            t2a[zq, zh, my] + r2a[0, n].astype(F32) + r2a[1, n].astype(F32) + r2a[2, n].astype(F32)
        )
        if n:
            a3_copy(n).start()
    for i in range(3):
        c2_copy(i).wait_recv()
    t3c[...] = t2c[mx] + r2c[0].astype(F32) + r2c[1].astype(F32) + r2c[2].astype(F32)
    for d in (1, 3, 2):
        c3_copy(d).start()

    for copy in sb_copies:
        copy.wait_recv()
    gsum = sb[0]
    for i in range(1, STRIPS):
        gsum = gsum + sb[i]
    gx[...] = gsum
    g1 = [remote(gx, gxr.at[d - 1], g_send.at[d - 1], g_recv.at[d - 1], on_x[d - 1]) for d in (1, 2, 3)]
    for copy in g1:
        copy.start()

    order = ((0, 1), (0, 3), (1, 0), (0, 2), (1, 1), (1, 3), (1, 2))

    def gat_copy(part, dz, dx):
        mine = gat.at[core, zlo, mx, part]
        target = place(x_peer(dx), my, zhi * 2 + lax.rem(zlo + dz, 2), core)
        return remote(mine, mine, gat_send.at[part, dz * 4 + dx], gat_recv.at[part, dz * 4 + dx], target)

    def mate_gat(part, dz, dx):
        block = gat.at[core, lax.rem(zlo + dz, 2), lax.rem(mx + 4 - dx, 4), part]
        return remote(block, block, fwd_send.at[part, dz * 4 + dx], fwd_recv.at[part, dz * 4 + dx], on_core)

    def assemble(c, part, dz, dx):
        zq = lax.rem(zlo + dz, 2)
        xq = lax.rem(mx + 4 - dx, 4)
        b = c * 8 + xq * 2 + zq

        @pl.when(b < BLOCKS)
        def _():
            k = part * 3 + lax.div(b, 5)
            j = lax.rem(b, 5)
            dwv[j, pl.ds(k, CI, stride=9), :] = gat[c, zq, xq, part].astype(F32)

    for part, third in ((1, b3_copy), (0, a3_copy), (2, c3_copy)):
        for d in (1, 2, 3):
            third(d).wait_recv()
        own = (t3a[zlo, zhi], t3b[mx], t3c[my])[part]
        gat[core, zlo, mx, part] = (own + r3[part, 0] + r3[part, 1] + r3[part, 2]).astype(BF16)
        for dz, dx in order:
            gat_copy(part, dz, dx).start()
        mate_gat(part, 0, 0).start()

    weighed = gsum * gamma
    row8 = lax.broadcasted_iota(jnp.int32, (8, C), 0)
    weighed = jnp.where(row8 == 0, weighed[0:1], weighed[1:2])
    moments = to_channels(to_groups(weighed) * (1.0 / COUNT))
    second = moments[0:1]
    first = moments[1:2]

    for copy in g1:
        copy.wait_recv()
    gz[...] = gx[...] + gxr[0] + gxr[1] + gxr[2]
    g2 = remote(gz, gzr, g_send.at[3], g_recv.at[3], on_zlo)
    g2.start()

    def finish(i, carry):
        scaled = (x[i].astype(F32) - mean) * inverse
        grad = inverse * (dn[i] * gamma - first - scaled * second) + wpad[i + 1].astype(F32)
        df[0, i] = grad.astype(BF16)
        return carry

    lax.fori_loop(0, ROWS, finish, 0)

    for part in (1, 0, 2):
        assemble(core, part, 0, 0)
    for dz, dx in order:
        for part in (1, 0, 2):
            gat_copy(part, dz, dx).wait_recv()
            mate_gat(part, dz, dx).start()
    for dz, dx in order:
        for part in (1, 0, 2):
            assemble(core, part, dz, dx)
    g2.wait_recv()
    gc[...] = gz[...] + gzr[...]
    g3 = remote(gc, gcr, g_send.at[4], g_recv.at[4], on_core)
    g3.start()
    for dz, dx in ((0, 0),) + order:
        for part in (1, 0, 2):
            mate_gat(part, dz, dx).wait_recv()
            assemble(mate, part, dz, dx)
    g3.wait_recv()
    dg_ref[...] = gc[...] + gcr[...]

    for copy in st_copies + halo + [mate_w] + mate_edge + sb_copies + g1 + [g2, g3]:
        copy.wait_send()
    for part in range(3):
        mate_gat(part, 0, 0).wait_send()
        for dz, dx in order:
            gat_copy(part, dz, dx).wait_send()
            mate_gat(part, dz, dx).wait_send()
    for d in (1, 2, 3):
        a3_copy(d).wait_send()
        b3_copy(d).wait_send()
        c3_copy(d).wait_send()

    def drain(s, carry):
        mate_act(s * 2).wait_send()
        mate_act(s * 2 + 1).wait_send()
        for d in (1, 2, 3):
            y_copy(s, d).wait_send()
            z_copy(s, d).wait_send()
            a2_copy(s, d).wait_send()
            b2_copy(s, d).wait_send()

        @pl.when(s < 3)
        def _():
            x_copy(s).wait_send()
            c2_copy(s).wait_send()

        return carry

    lax.fori_loop(0, 4, drain, 0)


def shards(features, cotangent, mask, conv_weight, gamma, beta):
    anywhere = pl.BlockSpec(memory_space=pl.ANY)
    vmem = pl.BlockSpec(memory_space=pltpu.VMEM)
    dma = pltpu.SemaphoreType.DMA

    def buf(*shape, dtype=BF16):
        return pltpu.VMEM(shape, dtype)

    panel = (CI, 128)
    dfeatures, dweight, dgains = pl.pallas_call(
        kernel,
        out_shape=(
            buf(1, ROWS, W, C),
            buf(5, 9 * CI, 128, dtype=F32),
            buf(2, C, dtype=F32),
        ),
        in_specs=[anywhere] * 6,
        out_specs=(vmem, vmem, vmem),
        scratch_shapes=[
            buf(ROWS, W, dtype=jnp.int32),
            buf(C, dtype=F32),
            buf(C, dtype=F32),
            buf(ROWS, W, C),
            buf(ROWS, W, C),
            buf(ROWS + 2, W, C),
            buf(ROWS + 2, W, C),
            buf(CELLS + 2 * W, LANES),
            buf(CELLS + 2 * W, HALF),
            buf(C, K9),
            buf(C, CELLS),
            buf(C, CELLS),
            buf(ROWS, W, C, dtype=F32),
            buf(2, 2, 4, *panel, dtype=F32),
            buf(4, 2, 2, *panel, dtype=F32),
            buf(4, 4, *panel, dtype=F32),
            buf(3, 4, 2, 2, 4, *panel),
            buf(3, 2, 2, 4, *panel),
            buf(3, 4, 2, 2, *panel),
            buf(3, 4, 4, *panel),
            buf(2, 2, 4, *panel, dtype=F32),
            buf(4, 2, 2, *panel, dtype=F32),
            buf(4, 4, *panel, dtype=F32),
            buf(2, 2, 4, *panel),
            buf(4, 2, 2, *panel),
            buf(4, 4, *panel),
            buf(3, 4, *panel),
            buf(3, 4, *panel),
            buf(3, 4, *panel),
            buf(2, 2, *panel, dtype=F32),
            buf(4, *panel, dtype=F32),
            buf(4, *panel, dtype=F32),
            buf(3, 3, *panel, dtype=F32),
            buf(2, 2, 4, 3, *panel),
            buf(STRIPS, 2, C, dtype=F32),
            buf(STRIPS, 2, C, dtype=F32),
            buf(2, C, dtype=F32),
            buf(3, 2, C, dtype=F32),
            buf(2, C, dtype=F32),
            buf(2, C, dtype=F32),
            buf(2, C, dtype=F32),
            buf(2, C, dtype=F32),
            dma((5,)),
            dma((9,)),
            dma((7,)),
            dma((7,)),
            dma((7,)),
            dma((7,)),
            dma((2,)),
            dma((2,)),
            dma((1,)),
            dma((1,)),
            dma((ROWS,)),
            dma((ROWS,)),
            dma((2,)),
            dma((2,)),
            dma((3,)),
            dma((3,)),
            dma((4, 3)),
            dma((4, 3)),
            dma((4, 3)),
            dma((4, 3)),
            dma((4, 3)),
            dma((4, 3)),
            dma((4, 3)),
            dma((4, 3)),
            dma((3,)),
            dma((3,)),
            dma((3, 3)),
            dma((3, 3)),
            dma((3, 8)),
            dma((3, 8)),
            dma((3, 8)),
            dma((3, 8)),
            dma((5,)),
            dma((5,)),
        ],
        compiler_params=pltpu.CompilerParams(
            collective_id=0, has_side_effects=True, vmem_limit_bytes=56 * 1024 * 1024
        ),
        cost_estimate=pl.CostEstimate(flops=4 * CELLS * K9 * C, bytes_accessed=13_000_000, transcendentals=CELLS * C),
    )(features, cotangent, mask, conv_weight, gamma, beta)
    return dfeatures, jnp.concatenate([dweight[j] for j in range(5)], axis=1), dgains


def solution(mesh):
    placed = (
        P("dp", "tile", None, None),
        P("dp", "tile", None, None),
        P("dp", "tile", None),
        P(),
        P(),
        P(),
    )
    return jax.shard_map(
        shards,
        mesh=mesh,
        in_specs=placed,
        out_specs=(P("dp", "tile", None, None), P("tile", None), P()),
        check_vma=False,
    )
```

```python
import jax
import jax.numpy as jnp
from jax import lax
from jax.experimental import pallas as pl
from jax.experimental.pallas import tpu as pltpu
from jax.sharding import PartitionSpec as P

MESH = pl.DeviceIdType.MESH
BF16 = jnp.bfloat16
F32 = jnp.float32

G = 32
EPSILON = 1e-05
C = 640
PER_GROUP = C // G
ROWS = 8
W = 128
CELLS = ROWS * W
STRIPS = 8
K3 = 3 * C
LANES = 2048
HALF = LANES // 2
BLOCKS = K3 // 128
K9 = 9 * C
CI = C // STRIPS
COUNT = float(ROWS * STRIPS * W * PER_GROUP)
SUB = 512


def kernel(
    x_hbm, cot_hbm, mask_hbm, w_hbm, gamma_hbm, beta_hbm,
    df, dwv, dg_ref,
    mask_ref, gamma_ref, beta_ref, x, cot, wpad, wpad_m, cols, cols_m, wmat, act_t, act_m, dn,
    part_sum, own1, own2, s1, r1a, r1b, r1c, t2a, t2b, t2c, h2a, h2b, h2c, r2a, r2b, r2c, t3a, t3b, t3c, r3, gat,
    st, sb, gx, gxr, gz, gzr, gc, gcr,
    load_sem, w_sem,
    st_send, st_recv, sb_send, sb_recv, halo_send, halo_recv,
    wm_send, wm_recv, am_send, am_recv, hm_send, hm_recv,
    a1_send, a1_recv, b1_send, b1_recv, c1_send, c1_recv,
    a2_send, a2_recv, b2_send, b2_recv, c2_send, c2_recv, s3_send, s3_recv,
    gat_send, gat_recv, fwd_send, fwd_recv, g_send, g_recv,
):
    dp = lax.axis_index("dp")
    tile = lax.axis_index("tile")
    core = lax.rem(dp, 2)
    mx = lax.rem(lax.div(dp, 2), 4)
    zlo = lax.div(dp, 8)
    zhi = lax.div(tile, 4)
    my = lax.rem(tile, 4)
    mz = zhi * 2 + zlo
    mate = 1 - core

    def place(px, py, pz, pc):
        return {
            "dp": (lax.rem(pz, 2) * 4 + px) * 2 + pc,
            "tile": lax.div(pz, 2) * 4 + py,
        }

    def x_peer(d):
        return lax.rem(mx + d, 4)

    def y_peer(d):
        return lax.rem(my + d, 4)

    def z_peer(d):
        return lax.rem(mz + d, 4)

    def remote(src, dst, send, recv, device):
        return pltpu.make_async_remote_copy(
            src_ref=src, dst_ref=dst, send_sem=send, recv_sem=recv, device_id=device, device_id_type=MESH
        )

    on_x = [place(x_peer(d), my, mz, core) for d in (1, 2, 3)]
    on_y = [place(mx, y_peer(d), mz, core) for d in (1, 2, 3)]
    on_z = [place(mx, my, z_peer(d), core) for d in (1, 2, 3)]
    on_core = place(mx, my, mz, mate)
    on_zlo = place(mx, my, zhi * 2 + 1 - zlo, core)

    def on_tile(d):
        return {"dp": dp, "tile": lax.rem(tile + d, STRIPS)}

    load_x = pltpu.make_async_copy(x_hbm.at[0], x, load_sem.at[0])
    load_x.start()
    load_cot = pltpu.make_async_copy(cot_hbm.at[0], cot, load_sem.at[1])
    load_cot.start()
    load_mask = pltpu.make_async_copy(mask_hbm.at[0], mask_ref, load_sem.at[2])
    load_gamma = pltpu.make_async_copy(gamma_hbm, gamma_ref, load_sem.at[3])
    load_beta = pltpu.make_async_copy(beta_hbm, beta_ref, load_sem.at[4])
    for load in (load_mask, load_gamma, load_beta):
        load.start()
    loads_w = [
        pltpu.make_async_copy(w_hbm.at[k // 3, k % 3], wmat.at[:, k * C : (k + 1) * C], w_sem.at[k]) for k in range(9)
    ]

    barrier = pltpu.get_barrier_semaphore()
    for device in on_x + on_y + on_z + [on_core]:
        pl.semaphore_signal(barrier, inc=1, device_id=device, device_id_type=MESH)
    for d in (1, 2, 3):
        other = place(mx, y_peer(d), (1 - zhi) * 2 + zlo, core)
        pl.semaphore_signal(barrier, inc=1, device_id=other, device_id_type=MESH)
        other = place(x_peer(d), my, zhi * 2 + 1 - zlo, core)
        pl.semaphore_signal(barrier, inc=1, device_id=other, device_id_type=MESH)

    load_x.wait()

    def fold(value):
        return jnp.sum(value.reshape(W // 8, 8, C), axis=0)

    zeros8 = jnp.zeros((8, C), F32)
    total = lax.fori_loop(0, ROWS, lambda i, acc: acc + fold(x[i].astype(F32)), zeros8)
    total = jnp.sum(total, axis=0, keepdims=True)
    local_mean = total * (1.0 / CELLS)

    def add_squares(i, acc):
        centered = x[i].astype(F32) - local_mean
        return acc + fold(centered * centered)

    squares = jnp.sum(lax.fori_loop(0, ROWS, add_squares, zeros8), axis=0, keepdims=True)
    st[tile, 0:1] = total
    st[tile, 1:2] = squares
    pl.semaphore_wait(barrier, 16)
    st_copies = [remote(st.at[tile], st.at[tile], st_send.at[d - 1], st_recv.at[d - 1], on_tile(d)) for d in range(1, 8)]
    for copy in st_copies:
        copy.start()

    load_cot.wait()
    for load in (load_mask, load_gamma, load_beta):
        load.wait()
    for load in loads_w:
        load.start()
    factor = (1.0 + mask_ref[...].astype(F32)).T
    for i in range(ROWS):
        wpad[i + 1] = (cot[i].astype(F32) * factor[:, i : i + 1]).astype(BF16)
    halo = [
        remote(wpad.at[ROWS], wpad.at[0], halo_send.at[0], halo_recv.at[0], on_tile(1)),
        remote(wpad.at[1], wpad.at[ROWS + 1], halo_send.at[1], halo_recv.at[1], on_tile(7)),
    ]
    mate_w = remote(wpad.at[pl.ds(1, ROWS)], wpad_m.at[pl.ds(1, ROWS)], wm_send.at[0], wm_recv.at[0], on_core)
    mate_w.start()
    for copy in halo:
        copy.start()

    rowsw = lax.broadcasted_iota(jnp.int32, (W, C), 0)

    def shifts(value):
        value = value.astype(F32)
        ahead = jnp.where(rowsw == W - 1, 0.0, pltpu.roll(value, W - 1, 0))
        behind = jnp.where(rowsw == 0, 0.0, pltpu.roll(value, 1, 0))
        return ahead.astype(BF16), value.astype(BF16), behind.astype(BF16)

    def spread(r):
        rows = pl.ds(pl.multiple_of(r * W, W), W)
        for ox, shifted in enumerate(shifts(wpad[r])):
            cols[rows, ox * C : (ox + 1) * C] = shifted
        cols[rows, K3:] = jnp.zeros((W, LANES - K3), BF16)

    def spread_mate(r):
        rows = pl.ds(pl.multiple_of(r * W, W), W)
        ahead, middle, behind = shifts(wpad_m[r])
        split = HALF - C

        @pl.when(core == 0)
        def _():
            cols_m[rows, :C] = ahead
            cols_m[rows, C:] = middle[:, :split]

        @pl.when(core == 1)
        def _():
            cols_m[rows, : C - split] = middle[:, split:]
            cols_m[rows, C - split : 2 * C - split] = behind
            cols_m[rows, 2 * C - split :] = jnp.zeros((W, LANES - K3), BF16)

    def inner(step):
        def body(r, carry):
            step(r)
            return carry

        lax.fori_loop(1, ROWS + 1, body, 0)

    inner(spread)

    chan = lax.broadcasted_iota(jnp.int32, (C, 128), 0).astype(F32)
    group = lax.broadcasted_iota(jnp.int32, (C, 128), 1).astype(F32)
    member = jnp.where(jnp.floor((chan + 0.5) * (1.0 / PER_GROUP)) == group, 1.0, 0.0).astype(BF16)
    chan_t = lax.broadcasted_iota(jnp.int32, (128, C), 1).astype(F32)
    group_t = lax.broadcasted_iota(jnp.int32, (128, C), 0).astype(F32)
    member_t = jnp.where(jnp.floor((chan_t + 0.5) * (1.0 / PER_GROUP)) == group_t, 1.0, 0.0).astype(BF16)

    def in_parts(value):
        high = value.astype(BF16).astype(F32)
        middle = (value - high).astype(BF16).astype(F32)
        return jnp.concatenate([high, middle, value - high - middle], axis=0).astype(BF16)

    def times(value, table):
        product = jnp.dot(in_parts(value), table, preferred_element_type=F32)
        return product[0:8] + product[8:16] + product[16:24]

    def to_groups(value):
        return times(value, member)

    def to_channels(value):
        return times(value, member_t)

    for copy in st_copies:
        copy.wait_recv()
    sums = st[0]
    for i in range(1, STRIPS):
        sums = sums + st[i]
    mean = to_channels(to_groups(jnp.broadcast_to(sums[0:1], (8, C))) * (1.0 / COUNT))[0:1]
    apart = jnp.zeros((1, C), F32)
    for i in range(STRIPS):
        centered = st[i, 0:1] * (1.0 / CELLS) - mean
        apart = apart + centered * centered
    spread_sq = apart * float(CELLS) + sums[1:2]
    variance = to_groups(jnp.broadcast_to(spread_sq, (8, C))) * (1.0 / COUNT)
    inverse = to_channels(lax.rsqrt(variance + EPSILON))[0:1]
    gamma = gamma_ref[...].reshape(1, C)
    beta = beta_ref[...].reshape(1, C)

    def mate_act(i):
        block = pl.ds(pl.multiple_of(i * W, W), W)
        return remote(act_t.at[:, block], act_m.at[:, block], am_send.at[i], am_recv.at[i], on_core)

    def activate(i, carry):
        scaled = (x[i].astype(F32) - mean) * inverse
        normed = scaled * gamma + beta
        sig = 0.5 + 0.5 * jnp.tanh(0.5 * normed)
        act = normed * sig
        dn[i] = sig * (1.0 + normed * (1.0 - sig))
        act_t[:, pl.ds(pl.multiple_of(i * W, W), W)] = act.T.astype(BF16)
        mate_act(i).start()
        return carry

    lax.fori_loop(0, ROWS, activate, 0)

    for copy in halo:
        copy.wait_recv()

    @pl.when(tile == 0)
    def _():
        wpad[0] = jnp.zeros((W, C), BF16)

    @pl.when(tile == STRIPS - 1)
    def _():
        wpad[ROWS + 1] = jnp.zeros((W, C), BF16)

    mate_edge = [
        remote(wpad.at[r], wpad_m.at[r], hm_send.at[n], hm_recv.at[n], on_core) for n, r in enumerate((0, ROWS + 1))
    ]
    for copy in mate_edge:
        copy.start()
    spread(0)
    spread(ROWS + 1)
    mate_w.wait_recv()
    inner(spread_mate)
    for copy in mate_edge:
        copy.wait_recv()
    spread_mate(0)
    spread_mate(ROWS + 1)
    for i in range(ROWS):
        mate_act(i).wait_recv()

    def partial(part, xq):
        rows = pl.ds((2 - part) * W, CELLS)
        own = cols[rows, pl.ds(pl.multiple_of(core * HALF + xq * 256, 256), 256)]
        theirs = cols_m[rows, pl.ds(pl.multiple_of(xq * 256, 256), 256)]
        return jnp.dot(act_t[...], own, preferred_element_type=F32) + jnp.dot(
            act_m[...], theirs, preferred_element_type=F32
        )

    def turn(s):
        return jnp.where(s == 0, 2, jnp.where(s == 1, 1, jnp.where(s == 2, 3, 0)))

    def x_copy(s):
        xq = x_peer(turn(s))
        return remote(s1.at[0, xq], r1a.at[s], a1_send.at[s], a1_recv.at[s], place(xq, my, mz, core))

    def y_copy(s, d):
        xq = x_peer(turn(s))
        src = s1.at[1, xq, :, :, y_peer(d)]
        return remote(src, r1b.at[d - 1, xq], b1_send.at[s, d - 1], b1_recv.at[s, d - 1], on_y[d - 1])

    def z_copy(s, d):
        xq = x_peer(turn(s))
        src = s1.at[2, xq, lax.rem(z_peer(d), 2), lax.div(z_peer(d), 2)]
        return remote(src, r1c.at[d - 1, xq], c1_send.at[s, d - 1], c1_recv.at[s, d - 1], on_z[d - 1])

    def grad_step(s, carry):
        xq = x_peer(turn(s))
        for part in range(3):
            result = partial(part, xq)
            for b in range(2):
                piece = result[:, b * 128 : (b + 1) * 128].reshape(2, 4, CI, 128)
                part_sum[b] = piece
                s1[part, xq, b] = piece.astype(BF16)
            if part == 0:

                @pl.when(s < 3)
                def _():
                    x_copy(s).start()

            for d in (1, 3, 2):
                if part == 1:
                    y_copy(s, d).start()
                if part == 2:
                    z_copy(s, d).start()
            if part == 1:
                own1[xq] = part_sum[:, :, my]
            if part == 2:
                own2[xq] = part_sum[zlo, zhi]
            if part == 0:

                @pl.when(s == 3)
                def _():
                    t2a[...] = part_sum[...]
        return carry

    lax.fori_loop(0, 4, grad_step, 0)

    for load in loads_w:
        load.wait()

    def dactive_step(i, carry):
        s0, s1_ = carry
        dact = jnp.zeros((SUB, C), F32)
        for oy in range(3):
            window = cols[pl.ds(pl.multiple_of(i * SUB + (2 - oy) * W, W), SUB), :K3]
            dact = dact + lax.dot_general(
                window, wmat[:, oy * K3 : (oy + 1) * K3], (((1,), (1,)), ((), ())), preferred_element_type=F32
            )
        for j in range(SUB // W):
            r = i * (SUB // W) + j
            dnormed = dact[j * W : (j + 1) * W] * dn[r]
            dn[r] = dnormed
            scaled = (x[r].astype(F32) - mean) * inverse
            s0 = s0 + fold(dnormed)
            s1_ = s1_ + fold(dnormed * scaled)
        return s0, s1_

    def z_of(d):
        return lax.rem(z_peer(d), 2), lax.div(z_peer(d), 2)

    def b2_copy(i, d):
        xq = x_peer(turn(i))
        zq, zh = z_of(d)
        return remote(h2b.at[xq, zq, zh], r2b.at[d - 1, xq], b2_send.at[i, d - 1], b2_recv.at[i, d - 1], on_z[d - 1])

    def c2_copy(i):
        xq = x_peer(turn(i))
        return remote(h2c.at[xq], r2c.at[i], c2_send.at[i], c2_recv.at[i], place(xq, my, mz, core))

    def a2_copy(n, d):
        zq, zh = z_of(n)
        return remote(h2a.at[zq, zh, y_peer(d)], r2a.at[d - 1, n], a2_send.at[n, d - 1], a2_recv.at[n, d - 1], on_y[d - 1])

    def a3_copy(d):
        zq, zh = z_of(d)
        return remote(t3a.at[zq, zh], r3.at[0, d - 1], s3_send.at[0, d - 1], s3_recv.at[0, d - 1], on_z[d - 1])

    def b3_copy(d):
        return remote(t3b.at[x_peer(d)], r3.at[1, d - 1], s3_send.at[1, d - 1], s3_recv.at[1, d - 1], on_x[d - 1])

    def c3_copy(d):
        return remote(t3c.at[y_peer(d)], r3.at[2, d - 1], s3_send.at[2, d - 1], s3_recv.at[2, d - 1], on_y[d - 1])

    def first_bc(i):
        xq = x_peer(turn(i))
        for d in (1, 2, 3):
            y_copy(i, d).wait_recv()
        total = own1[xq] + r1b[0, xq].astype(F32) + r1b[1, xq].astype(F32) + r1b[2, xq].astype(F32)
        t2b[xq] = total
        h2b[xq] = total.astype(BF16)
        for d in (1, 3, 2):
            b2_copy(i, d).start()
        for d in (1, 2, 3):
            z_copy(i, d).wait_recv()
        total = own2[xq] + r1c[0, xq].astype(F32) + r1c[1, xq].astype(F32) + r1c[2, xq].astype(F32)
        t2c[xq] = total
        h2c[xq] = total.astype(BF16)
        if i < 3:
            c2_copy(i).start()

    def first_a():
        for i in range(3):
            x_copy(i).wait_recv()
        total = t2a[...] + r1a[0].astype(F32) + r1a[1].astype(F32) + r1a[2].astype(F32)
        t2a[...] = total
        h2a[...] = total.astype(BF16)
        for n in (1, 3, 2, 0):
            for d in (1, 3, 2):
                a2_copy(n, d).start()

    sums01 = (zeros8, zeros8)
    sums01 = dactive_step(0, sums01)
    first_bc(0)
    first_bc(1)
    first_bc(2)
    first_a()
    first_bc(3)
    sums01 = dactive_step(1, sums01)
    sum0 = jnp.sum(sums01[0], axis=0, keepdims=True)
    sum1 = jnp.sum(sums01[1], axis=0, keepdims=True)
    sb[tile, 0:1] = sum1
    sb[tile, 1:2] = sum0
    sb_copies = [remote(sb.at[tile], sb.at[tile], sb_send.at[d - 1], sb_recv.at[d - 1], on_tile(d)) for d in range(1, 8)]
    for copy in sb_copies:
        copy.start()

    for i, n in ((0, 2), (1, 1), (2, 3), (3, 0)):
        xq = x_peer(n)
        for d in (1, 2, 3):
            b2_copy(i, d).wait_recv()
        t3b[xq] = (
            t2b[xq, zlo, zhi] + r2b[0, xq].astype(F32) + r2b[1, xq].astype(F32) + r2b[2, xq].astype(F32)
        )
        if n:
            b3_copy(n).start()
        zq, zh = z_of(n)
        for d in (1, 2, 3):
            a2_copy(n, d).wait_recv()
        t3a[zq, zh] = (
            t2a[zq, zh, my] + r2a[0, n].astype(F32) + r2a[1, n].astype(F32) + r2a[2, n].astype(F32)
        )
        if n:
            a3_copy(n).start()
    for i in range(3):
        c2_copy(i).wait_recv()
    t3c[...] = t2c[mx] + r2c[0].astype(F32) + r2c[1].astype(F32) + r2c[2].astype(F32)
    for d in (1, 3, 2):
        c3_copy(d).start()

    for copy in sb_copies:
        copy.wait_recv()
    gsum = sb[0]
    for i in range(1, STRIPS):
        gsum = gsum + sb[i]
    gx[...] = gsum
    g1 = [remote(gx, gxr.at[d - 1], g_send.at[d - 1], g_recv.at[d - 1], on_x[d - 1]) for d in (1, 2, 3)]
    for copy in g1:
        copy.start()

    order = ((0, 1), (0, 3), (1, 0), (0, 2), (1, 1), (1, 3), (1, 2))

    def gat_copy(part, dz, dx):
        mine = gat.at[core, zlo, mx, part]
        target = place(x_peer(dx), my, zhi * 2 + lax.rem(zlo + dz, 2), core)
        return remote(mine, mine, gat_send.at[part, dz * 4 + dx], gat_recv.at[part, dz * 4 + dx], target)

    def mate_gat(part, dz, dx):
        block = gat.at[core, lax.rem(zlo + dz, 2), lax.rem(mx + 4 - dx, 4), part]
        return remote(block, block, fwd_send.at[part, dz * 4 + dx], fwd_recv.at[part, dz * 4 + dx], on_core)

    def assemble(c, part, dz, dx):
        zq = lax.rem(zlo + dz, 2)
        xq = lax.rem(mx + 4 - dx, 4)
        b = c * 8 + xq * 2 + zq

        @pl.when(b < BLOCKS)
        def _():
            k = part * 3 + lax.div(b, 5)
            j = lax.rem(b, 5)
            dwv[j, pl.ds(k, CI, stride=9), :] = gat[c, zq, xq, part].astype(F32)

    for part, third in ((1, b3_copy), (0, a3_copy), (2, c3_copy)):
        for d in (1, 2, 3):
            third(d).wait_recv()
        own = (t3a[zlo, zhi], t3b[mx], t3c[my])[part]
        gat[core, zlo, mx, part] = (own + r3[part, 0] + r3[part, 1] + r3[part, 2]).astype(BF16)
        for dz, dx in order:
            gat_copy(part, dz, dx).start()
        mate_gat(part, 0, 0).start()

    weighed = gsum * gamma
    row8 = lax.broadcasted_iota(jnp.int32, (8, C), 0)
    weighed = jnp.where(row8 == 0, weighed[0:1], weighed[1:2])
    moments = to_channels(to_groups(weighed) * (1.0 / COUNT))
    second = moments[0:1]
    first = moments[1:2]

    for copy in g1:
        copy.wait_recv()
    gz[...] = gx[...] + gxr[0] + gxr[1] + gxr[2]
    g2 = remote(gz, gzr, g_send.at[3], g_recv.at[3], on_zlo)
    g2.start()

    def finish(i, carry):
        scaled = (x[i].astype(F32) - mean) * inverse
        grad = inverse * (dn[i] * gamma - first - scaled * second) + wpad[i + 1].astype(F32)
        df[0, i] = grad.astype(BF16)
        return carry

    lax.fori_loop(0, ROWS, finish, 0)

    for part in (1, 0, 2):
        assemble(core, part, 0, 0)
    for dz, dx in order:
        for part in (1, 0, 2):
            gat_copy(part, dz, dx).wait_recv()
            mate_gat(part, dz, dx).start()
    for dz, dx in order:
        for part in (1, 0, 2):
            assemble(core, part, dz, dx)
    g2.wait_recv()
    gc[...] = gz[...] + gzr[...]
    g3 = remote(gc, gcr, g_send.at[4], g_recv.at[4], on_core)
    g3.start()
    for dz, dx in ((0, 0),) + order:
        for part in (1, 0, 2):
            mate_gat(part, dz, dx).wait_recv()
            assemble(mate, part, dz, dx)
    g3.wait_recv()
    dg_ref[...] = gc[...] + gcr[...]

    for copy in st_copies + halo + [mate_w] + mate_edge + sb_copies + g1 + [g2, g3]:
        copy.wait_send()
    for part in range(3):
        mate_gat(part, 0, 0).wait_send()
        for dz, dx in order:
            gat_copy(part, dz, dx).wait_send()
            mate_gat(part, dz, dx).wait_send()
    for d in (1, 2, 3):
        a3_copy(d).wait_send()
        b3_copy(d).wait_send()
        c3_copy(d).wait_send()

    def drain(s, carry):
        mate_act(s * 2).wait_send()
        mate_act(s * 2 + 1).wait_send()
        for d in (1, 2, 3):
            y_copy(s, d).wait_send()
            z_copy(s, d).wait_send()
            a2_copy(s, d).wait_send()
            b2_copy(s, d).wait_send()

        @pl.when(s < 3)
        def _():
            x_copy(s).wait_send()
            c2_copy(s).wait_send()

        return carry

    lax.fori_loop(0, 4, drain, 0)


def shards(features, cotangent, mask, conv_weight, gamma, beta):
    anywhere = pl.BlockSpec(memory_space=pl.ANY)
    vmem = pl.BlockSpec(memory_space=pltpu.VMEM)
    dma = pltpu.SemaphoreType.DMA

    def buf(*shape, dtype=BF16):
        return pltpu.VMEM(shape, dtype)

    panel = (CI, 128)
    dfeatures, dweight, dgains = pl.pallas_call(
        kernel,
        out_shape=(
            buf(1, ROWS, W, C),
            buf(5, 9 * CI + 8, 128, dtype=F32),
            buf(2, C, dtype=F32),
        ),
        in_specs=[anywhere] * 6,
        out_specs=(vmem, vmem, vmem),
        scratch_shapes=[
            buf(ROWS, W, dtype=jnp.int32),
            buf(C, dtype=F32),
            buf(C, dtype=F32),
            buf(ROWS, W, C),
            buf(ROWS, W, C),
            buf(ROWS + 2, W, C),
            buf(ROWS + 2, W, C),
            buf(CELLS + 2 * W, LANES),
            buf(CELLS + 2 * W, HALF),
            buf(C, K9),
            buf(C, CELLS),
            buf(C, CELLS),
            buf(ROWS, W, C, dtype=F32),
            buf(2, 2, 4, *panel, dtype=F32),
            buf(4, 2, 2, *panel, dtype=F32),
            buf(4, 4, *panel, dtype=F32),
            buf(3, 4, 2, 2, 4, *panel),
            buf(3, 2, 2, 4, *panel),
            buf(3, 4, 2, 2, *panel),
            buf(3, 4, 4, *panel),
            buf(2, 2, 4, *panel, dtype=F32),
            buf(4, 2, 2, *panel, dtype=F32),
            buf(4, 4, *panel, dtype=F32),
            buf(2, 2, 4, *panel),
            buf(4, 2, 2, *panel),
            buf(4, 4, *panel),
            buf(3, 4, *panel),
            buf(3, 4, *panel),
            buf(3, 4, *panel),
            buf(2, 2, *panel, dtype=F32),
            buf(4, *panel, dtype=F32),
            buf(4, *panel, dtype=F32),
            buf(3, 3, *panel, dtype=F32),
            buf(2, 2, 4, 3, *panel),
            buf(STRIPS, 2, C, dtype=F32),
            buf(STRIPS, 2, C, dtype=F32),
            buf(2, C, dtype=F32),
            buf(3, 2, C, dtype=F32),
            buf(2, C, dtype=F32),
            buf(2, C, dtype=F32),
            buf(2, C, dtype=F32),
            buf(2, C, dtype=F32),
            dma((5,)),
            dma((9,)),
            dma((7,)),
            dma((7,)),
            dma((7,)),
            dma((7,)),
            dma((2,)),
            dma((2,)),
            dma((1,)),
            dma((1,)),
            dma((ROWS,)),
            dma((ROWS,)),
            dma((2,)),
            dma((2,)),
            dma((3,)),
            dma((3,)),
            dma((4, 3)),
            dma((4, 3)),
            dma((4, 3)),
            dma((4, 3)),
            dma((4, 3)),
            dma((4, 3)),
            dma((4, 3)),
            dma((4, 3)),
            dma((3,)),
            dma((3,)),
            dma((3, 3)),
            dma((3, 3)),
            dma((3, 8)),
            dma((3, 8)),
            dma((3, 8)),
            dma((3, 8)),
            dma((5,)),
            dma((5,)),
        ],
        compiler_params=pltpu.CompilerParams(
            collective_id=0, has_side_effects=True, vmem_limit_bytes=56 * 1024 * 1024
        ),
        cost_estimate=pl.CostEstimate(flops=4 * CELLS * K9 * C, bytes_accessed=13_000_000, transcendentals=CELLS * C),
    )(features, cotangent, mask, conv_weight, gamma, beta)
    return dfeatures, jnp.concatenate([dweight[j, : 9 * CI] for j in range(5)], axis=1), dgains


def solution(mesh):
    placed = (
        P("dp", "tile", None, None),
        P("dp", "tile", None, None),
        P("dp", "tile", None),
        P(),
        P(),
        P(),
    )
    return jax.shard_map(
        shards,
        mesh=mesh,
        in_specs=placed,
        out_specs=(P("dp", "tile", None, None), P("tile", None), P()),
        check_vma=False,
    )
```

```python
import jax
import jax.numpy as jnp
from jax import lax
from jax.experimental import pallas as pl
from jax.experimental.pallas import tpu as pltpu
from jax.sharding import PartitionSpec as P

MESH = pl.DeviceIdType.MESH
BF16 = jnp.bfloat16
F32 = jnp.float32

G = 32
EPSILON = 1e-05
C = 640
PER_GROUP = C // G
ROWS = 8
W = 128
CELLS = ROWS * W
STRIPS = 8
K3 = 3 * C
LANES = 2048
HALF = LANES // 2
BLOCKS = K3 // 128
K9 = 9 * C
CI = C // STRIPS
COUNT = float(ROWS * STRIPS * W * PER_GROUP)
SUB = 512


def kernel(
    x_hbm, cot_hbm, mask_hbm, w_hbm, gamma_hbm, beta_hbm,
    df, dwv, dg_ref,
    mask_ref, gamma_ref, beta_ref, x, cot, wpad, wpad_m, cols, cols_m, wmat, act_t, act_m, dn,
    part_sum, own1, own2, s1, r1a, r1b, r1c, t2a, t2b, t2c, h2a, h2b, h2c, r2a, r2b, r2c, t3a, t3b, t3c, r3, gat,
    st, sb, gx, gc, gcr,
    load_sem, w_sem,
    st_send, st_recv, sb_send, sb_recv, halo_send, halo_recv,
    wm_send, wm_recv, am_send, am_recv, hm_send, hm_recv,
    a1_send, a1_recv, b1_send, b1_recv, c1_send, c1_recv,
    a2_send, a2_recv, b2_send, b2_recv, c2_send, c2_recv, s3_send, s3_recv,
    gat_send, gat_recv, fwd_send, fwd_recv, g_send, g_recv,
):
    dp = lax.axis_index("dp")
    tile = lax.axis_index("tile")
    core = lax.rem(dp, 2)
    mx = lax.rem(lax.div(dp, 2), 4)
    zlo = lax.div(dp, 8)
    zhi = lax.div(tile, 4)
    my = lax.rem(tile, 4)
    mz = zhi * 2 + zlo
    mate = 1 - core

    def place(px, py, pz, pc):
        return {
            "dp": (lax.rem(pz, 2) * 4 + px) * 2 + pc,
            "tile": lax.div(pz, 2) * 4 + py,
        }

    def x_peer(d):
        return lax.rem(mx + d, 4)

    def y_peer(d):
        return lax.rem(my + d, 4)

    def z_peer(d):
        return lax.rem(mz + d, 4)

    def remote(src, dst, send, recv, device):
        return pltpu.make_async_remote_copy(
            src_ref=src, dst_ref=dst, send_sem=send, recv_sem=recv, device_id=device, device_id_type=MESH
        )

    on_x = [place(x_peer(d), my, mz, core) for d in (1, 2, 3)]
    on_y = [place(mx, y_peer(d), mz, core) for d in (1, 2, 3)]
    on_z = [place(mx, my, z_peer(d), core) for d in (1, 2, 3)]
    on_core = place(mx, my, mz, mate)

    def on_tile(d):
        return {"dp": dp, "tile": lax.rem(tile + d, STRIPS)}

    load_x = pltpu.make_async_copy(x_hbm.at[0], x, load_sem.at[0])
    load_x.start()
    load_cot = pltpu.make_async_copy(cot_hbm.at[0], cot, load_sem.at[1])
    load_cot.start()
    load_mask = pltpu.make_async_copy(mask_hbm.at[0], mask_ref, load_sem.at[2])
    load_gamma = pltpu.make_async_copy(gamma_hbm, gamma_ref, load_sem.at[3])
    load_beta = pltpu.make_async_copy(beta_hbm, beta_ref, load_sem.at[4])
    for load in (load_mask, load_gamma, load_beta):
        load.start()
    loads_w = [
        pltpu.make_async_copy(w_hbm.at[k // 3, k % 3], wmat.at[:, k * C : (k + 1) * C], w_sem.at[k]) for k in range(9)
    ]

    barrier = pltpu.get_barrier_semaphore()
    for device in on_x + on_y + on_z + [on_core]:
        pl.semaphore_signal(barrier, inc=1, device_id=device, device_id_type=MESH)
    for d in (1, 2, 3):
        other = place(mx, y_peer(d), (1 - zhi) * 2 + zlo, core)
        pl.semaphore_signal(barrier, inc=1, device_id=other, device_id_type=MESH)
        other = place(x_peer(d), my, zhi * 2 + 1 - zlo, core)
        pl.semaphore_signal(barrier, inc=1, device_id=other, device_id_type=MESH)

    load_x.wait()

    def fold(value):
        return jnp.sum(value.reshape(W // 8, 8, C), axis=0)

    zeros8 = jnp.zeros((8, C), F32)
    total = lax.fori_loop(0, ROWS, lambda i, acc: acc + fold(x[i].astype(F32)), zeros8)
    total = jnp.sum(total, axis=0, keepdims=True)
    local_mean = total * (1.0 / CELLS)

    def add_squares(i, acc):
        centered = x[i].astype(F32) - local_mean
        return acc + fold(centered * centered)

    squares = jnp.sum(lax.fori_loop(0, ROWS, add_squares, zeros8), axis=0, keepdims=True)
    st[tile, 0:1] = total
    st[tile, 1:2] = squares
    pl.semaphore_wait(barrier, 16)
    st_copies = [remote(st.at[tile], st.at[tile], st_send.at[d - 1], st_recv.at[d - 1], on_tile(d)) for d in range(1, 8)]
    for copy in st_copies:
        copy.start()

    load_cot.wait()
    for load in (load_mask, load_gamma, load_beta):
        load.wait()
    for load in loads_w:
        load.start()
    factor = (1.0 + mask_ref[...].astype(F32)).T
    for i in range(ROWS):
        wpad[i + 1] = (cot[i].astype(F32) * factor[:, i : i + 1]).astype(BF16)
    halo = [
        remote(wpad.at[ROWS], wpad.at[0], halo_send.at[0], halo_recv.at[0], on_tile(1)),
        remote(wpad.at[1], wpad.at[ROWS + 1], halo_send.at[1], halo_recv.at[1], on_tile(7)),
    ]
    mate_w = remote(wpad.at[pl.ds(1, ROWS)], wpad_m.at[pl.ds(1, ROWS)], wm_send.at[0], wm_recv.at[0], on_core)
    mate_w.start()
    for copy in halo:
        copy.start()

    rowsw = lax.broadcasted_iota(jnp.int32, (W, C), 0)

    def shifts(value):
        value = value.astype(F32)
        ahead = jnp.where(rowsw == W - 1, 0.0, pltpu.roll(value, W - 1, 0))
        behind = jnp.where(rowsw == 0, 0.0, pltpu.roll(value, 1, 0))
        return ahead.astype(BF16), value.astype(BF16), behind.astype(BF16)

    def spread(r):
        rows = pl.ds(pl.multiple_of(r * W, W), W)
        for ox, shifted in enumerate(shifts(wpad[r])):
            cols[rows, ox * C : (ox + 1) * C] = shifted
        cols[rows, K3:] = jnp.zeros((W, LANES - K3), BF16)

    def spread_mate(r):
        rows = pl.ds(pl.multiple_of(r * W, W), W)
        ahead, middle, behind = shifts(wpad_m[r])
        split = HALF - C

        @pl.when(core == 0)
        def _():
            cols_m[rows, :C] = ahead
            cols_m[rows, C:] = middle[:, :split]

        @pl.when(core == 1)
        def _():
            cols_m[rows, : C - split] = middle[:, split:]
            cols_m[rows, C - split : 2 * C - split] = behind
            cols_m[rows, 2 * C - split :] = jnp.zeros((W, LANES - K3), BF16)

    def inner(step):
        def body(r, carry):
            step(r)
            return carry

        lax.fori_loop(1, ROWS + 1, body, 0)

    inner(spread)

    chan = lax.broadcasted_iota(jnp.int32, (C, 128), 0).astype(F32)
    group = lax.broadcasted_iota(jnp.int32, (C, 128), 1).astype(F32)
    member = jnp.where(jnp.floor((chan + 0.5) * (1.0 / PER_GROUP)) == group, 1.0, 0.0).astype(BF16)
    chan_t = lax.broadcasted_iota(jnp.int32, (128, C), 1).astype(F32)
    group_t = lax.broadcasted_iota(jnp.int32, (128, C), 0).astype(F32)
    member_t = jnp.where(jnp.floor((chan_t + 0.5) * (1.0 / PER_GROUP)) == group_t, 1.0, 0.0).astype(BF16)

    def in_parts(value):
        high = value.astype(BF16).astype(F32)
        middle = (value - high).astype(BF16).astype(F32)
        return jnp.concatenate([high, middle, value - high - middle], axis=0).astype(BF16)

    def times(value, table):
        product = jnp.dot(in_parts(value), table, preferred_element_type=F32)
        return product[0:8] + product[8:16] + product[16:24]

    def to_groups(value):
        return times(value, member)

    def to_channels(value):
        return times(value, member_t)

    for copy in st_copies:
        copy.wait_recv()
    sums = st[0]
    for i in range(1, STRIPS):
        sums = sums + st[i]
    mean = to_channels(to_groups(jnp.broadcast_to(sums[0:1], (8, C))) * (1.0 / COUNT))[0:1]
    apart = jnp.zeros((1, C), F32)
    for i in range(STRIPS):
        centered = st[i, 0:1] * (1.0 / CELLS) - mean
        apart = apart + centered * centered
    spread_sq = apart * float(CELLS) + sums[1:2]
    variance = to_groups(jnp.broadcast_to(spread_sq, (8, C))) * (1.0 / COUNT)
    inverse = to_channels(lax.rsqrt(variance + EPSILON))[0:1]
    gamma = gamma_ref[...].reshape(1, C)
    beta = beta_ref[...].reshape(1, C)

    def mate_act(i):
        block = pl.ds(pl.multiple_of(i * W, W), W)
        return remote(act_t.at[:, block], act_m.at[:, block], am_send.at[i], am_recv.at[i], on_core)

    def activate(i, carry):
        scaled = (x[i].astype(F32) - mean) * inverse
        normed = scaled * gamma + beta
        sig = 0.5 + 0.5 * jnp.tanh(0.5 * normed)
        act = normed * sig
        dn[i] = sig * (1.0 + normed * (1.0 - sig))
        act_t[:, pl.ds(pl.multiple_of(i * W, W), W)] = act.T.astype(BF16)
        mate_act(i).start()
        return carry

    lax.fori_loop(0, ROWS, activate, 0)

    for copy in halo:
        copy.wait_recv()

    @pl.when(tile == 0)
    def _():
        wpad[0] = jnp.zeros((W, C), BF16)

    @pl.when(tile == STRIPS - 1)
    def _():
        wpad[ROWS + 1] = jnp.zeros((W, C), BF16)

    mate_edge = [
        remote(wpad.at[r], wpad_m.at[r], hm_send.at[n], hm_recv.at[n], on_core) for n, r in enumerate((0, ROWS + 1))
    ]
    for copy in mate_edge:
        copy.start()
    spread(0)
    spread(ROWS + 1)
    mate_w.wait_recv()
    inner(spread_mate)
    for copy in mate_edge:
        copy.wait_recv()
    spread_mate(0)
    spread_mate(ROWS + 1)
    for i in range(ROWS):
        mate_act(i).wait_recv()

    def partial(part, xq):
        rows = pl.ds((2 - part) * W, CELLS)
        own = cols[rows, pl.ds(pl.multiple_of(core * HALF + xq * 256, 256), 256)]
        theirs = cols_m[rows, pl.ds(pl.multiple_of(xq * 256, 256), 256)]
        return jnp.dot(act_t[...], own, preferred_element_type=F32) + jnp.dot(
            act_m[...], theirs, preferred_element_type=F32
        )

    def turn(s):
        return jnp.where(s == 0, 2, jnp.where(s == 1, 1, jnp.where(s == 2, 3, 0)))

    def x_copy(s):
        xq = x_peer(turn(s))
        return remote(s1.at[0, xq], r1a.at[s], a1_send.at[s], a1_recv.at[s], place(xq, my, mz, core))

    def y_copy(s, d):
        xq = x_peer(turn(s))
        src = s1.at[1, xq, :, :, y_peer(d)]
        return remote(src, r1b.at[d - 1, xq], b1_send.at[s, d - 1], b1_recv.at[s, d - 1], on_y[d - 1])

    def z_copy(s, d):
        xq = x_peer(turn(s))
        src = s1.at[2, xq, lax.rem(z_peer(d), 2), lax.div(z_peer(d), 2)]
        return remote(src, r1c.at[d - 1, xq], c1_send.at[s, d - 1], c1_recv.at[s, d - 1], on_z[d - 1])

    def grad_step(s, carry):
        xq = x_peer(turn(s))
        for part in range(3):
            result = partial(part, xq)
            for b in range(2):
                piece = result[:, b * 128 : (b + 1) * 128].reshape(2, 4, CI, 128)
                part_sum[b] = piece
                s1[part, xq, b] = piece.astype(BF16)
            if part == 0:

                @pl.when(s < 3)
                def _():
                    x_copy(s).start()

            for d in (1, 3, 2):
                if part == 1:
                    y_copy(s, d).start()
                if part == 2:
                    z_copy(s, d).start()
            if part == 1:
                own1[xq] = part_sum[:, :, my]
            if part == 2:
                own2[xq] = part_sum[zlo, zhi]
            if part == 0:

                @pl.when(s == 3)
                def _():
                    t2a[...] = part_sum[...]
        return carry

    lax.fori_loop(0, 4, grad_step, 0)

    for load in loads_w:
        load.wait()

    def dactive_step(i, carry):
        s0, s1_ = carry
        dact = jnp.zeros((SUB, C), F32)
        for oy in range(3):
            window = cols[pl.ds(pl.multiple_of(i * SUB + (2 - oy) * W, W), SUB), :K3]
            dact = dact + lax.dot_general(
                window, wmat[:, oy * K3 : (oy + 1) * K3], (((1,), (1,)), ((), ())), preferred_element_type=F32
            )
        for j in range(SUB // W):
            r = i * (SUB // W) + j
            dnormed = dact[j * W : (j + 1) * W] * dn[r]
            dn[r] = dnormed
            scaled = (x[r].astype(F32) - mean) * inverse
            s0 = s0 + fold(dnormed)
            s1_ = s1_ + fold(dnormed * scaled)
        return s0, s1_

    def z_of(d):
        return lax.rem(z_peer(d), 2), lax.div(z_peer(d), 2)

    def b2_copy(i, d):
        xq = x_peer(turn(i))
        zq, zh = z_of(d)
        return remote(h2b.at[xq, zq, zh], r2b.at[d - 1, xq], b2_send.at[i, d - 1], b2_recv.at[i, d - 1], on_z[d - 1])

    def c2_copy(i):
        xq = x_peer(turn(i))
        return remote(h2c.at[xq], r2c.at[i], c2_send.at[i], c2_recv.at[i], place(xq, my, mz, core))

    def a2_copy(n, d):
        zq, zh = z_of(n)
        return remote(h2a.at[zq, zh, y_peer(d)], r2a.at[d - 1, n], a2_send.at[n, d - 1], a2_recv.at[n, d - 1], on_y[d - 1])

    def a3_copy(d):
        zq, zh = z_of(d)
        return remote(t3a.at[zq, zh], r3.at[0, d - 1], s3_send.at[0, d - 1], s3_recv.at[0, d - 1], on_z[d - 1])

    def b3_copy(d):
        return remote(t3b.at[x_peer(d)], r3.at[1, d - 1], s3_send.at[1, d - 1], s3_recv.at[1, d - 1], on_x[d - 1])

    def c3_copy(d):
        return remote(t3c.at[y_peer(d)], r3.at[2, d - 1], s3_send.at[2, d - 1], s3_recv.at[2, d - 1], on_y[d - 1])

    def first_bc(i):
        xq = x_peer(turn(i))
        for d in (1, 2, 3):
            y_copy(i, d).wait_recv()
        total = own1[xq] + r1b[0, xq].astype(F32) + r1b[1, xq].astype(F32) + r1b[2, xq].astype(F32)
        t2b[xq] = total
        h2b[xq] = total.astype(BF16)
        for d in (1, 3, 2):
            b2_copy(i, d).start()
        for d in (1, 2, 3):
            z_copy(i, d).wait_recv()
        total = own2[xq] + r1c[0, xq].astype(F32) + r1c[1, xq].astype(F32) + r1c[2, xq].astype(F32)
        t2c[xq] = total
        h2c[xq] = total.astype(BF16)
        if i < 3:
            c2_copy(i).start()

    def first_sent(s):
        mate_act(s * 4).wait_send()
        mate_act(s * 4 + 1).wait_send()
        mate_act(s * 4 + 2).wait_send()
        mate_act(s * 4 + 3).wait_send()
        x_copy(s).wait_send()
        for d in (1, 2, 3):
            y_copy(s, d).wait_send()
            z_copy(s, d).wait_send()

    def first_a():
        for i in range(3):
            x_copy(i).wait_recv()
        total = t2a[...] + r1a[0].astype(F32) + r1a[1].astype(F32) + r1a[2].astype(F32)
        t2a[...] = total
        h2a[...] = total.astype(BF16)
        for n in (1, 3, 2, 0):
            for d in (1, 3, 2):
                a2_copy(n, d).start()

    sums01 = (zeros8, zeros8)
    sums01 = dactive_step(0, sums01)
    first_bc(0)
    first_bc(1)
    for copy in st_copies + halo + [mate_w] + mate_edge:
        copy.wait_send()
    for s in range(2):
        first_sent(s)
    first_bc(2)
    first_a()
    first_bc(3)
    sums01 = dactive_step(1, sums01)
    sum0 = jnp.sum(sums01[0], axis=0, keepdims=True)
    sum1 = jnp.sum(sums01[1], axis=0, keepdims=True)
    sb[tile, 0:1] = sum1
    sb[tile, 1:2] = sum0
    sb_copies = [remote(sb.at[tile], sb.at[tile], sb_send.at[d - 1], sb_recv.at[d - 1], on_tile(d)) for d in range(1, 8)]
    for copy in sb_copies:
        copy.start()

    for i, n in ((0, 2), (1, 1), (2, 3), (3, 0)):
        xq = x_peer(n)
        for d in (1, 2, 3):
            b2_copy(i, d).wait_recv()
        t3b[xq] = (
            t2b[xq, zlo, zhi] + r2b[0, xq].astype(F32) + r2b[1, xq].astype(F32) + r2b[2, xq].astype(F32)
        )
        if n:
            b3_copy(n).start()
        zq, zh = z_of(n)
        for d in (1, 2, 3):
            a2_copy(n, d).wait_recv()
        t3a[zq, zh] = (
            t2a[zq, zh, my] + r2a[0, n].astype(F32) + r2a[1, n].astype(F32) + r2a[2, n].astype(F32)
        )
        if n:
            a3_copy(n).start()
    for i in range(3):
        c2_copy(i).wait_recv()
    t3c[...] = t2c[mx] + r2c[0].astype(F32) + r2c[1].astype(F32) + r2c[2].astype(F32)
    for d in (1, 3, 2):
        c3_copy(d).start()

    order = ((0, 1), (0, 3), (1, 0), (0, 2), (1, 1), (1, 3), (1, 2))

    for copy in sb_copies:
        copy.wait_recv()
    gsum = sb[0]
    for i in range(1, STRIPS):
        gsum = gsum + sb[i]
    gx[zlo, mx] = gsum
    g1 = []
    for n, (dz, dx) in enumerate(order):
        target = place(x_peer(dx), my, zhi * 2 + lax.rem(zlo + dz, 2), core)
        g1.append(remote(gx.at[zlo, mx], gx.at[zlo, mx], g_send.at[n], g_recv.at[n], target))
    for copy in g1:
        copy.start()


    def gat_copy(part, dz, dx):
        mine = gat.at[core, zlo, mx, part]
        target = place(x_peer(dx), my, zhi * 2 + lax.rem(zlo + dz, 2), core)
        return remote(mine, mine, gat_send.at[part, dz * 4 + dx], gat_recv.at[part, dz * 4 + dx], target)

    def mate_gat(part, dz, dx):
        block = gat.at[core, lax.rem(zlo + dz, 2), lax.rem(mx + 4 - dx, 4), part]
        return remote(block, block, fwd_send.at[part, dz * 4 + dx], fwd_recv.at[part, dz * 4 + dx], on_core)

    def assemble(c, part, dz, dx):
        zq = lax.rem(zlo + dz, 2)
        xq = lax.rem(mx + 4 - dx, 4)
        b = c * 8 + xq * 2 + zq

        @pl.when(b < BLOCKS)
        def _():
            k = part * 3 + lax.div(b, 5)
            j = lax.rem(b, 5)
            dwv[j, pl.ds(k, CI, stride=9), :] = gat[c, zq, xq, part].astype(F32)

    for part, third in ((1, b3_copy), (0, a3_copy), (2, c3_copy)):
        for d in (1, 2, 3):
            third(d).wait_recv()
        own = (t3a[zlo, zhi], t3b[mx], t3c[my])[part]
        gat[core, zlo, mx, part] = (own + r3[part, 0] + r3[part, 1] + r3[part, 2]).astype(BF16)
        for dz, dx in order:
            gat_copy(part, dz, dx).start()
        mate_gat(part, 0, 0).start()

    weighed = gsum * gamma
    row8 = lax.broadcasted_iota(jnp.int32, (8, C), 0)
    weighed = jnp.where(row8 == 0, weighed[0:1], weighed[1:2])
    moments = to_channels(to_groups(weighed) * (1.0 / COUNT))
    second = moments[0:1]
    first = moments[1:2]

    def finish(i, carry):
        scaled = (x[i].astype(F32) - mean) * inverse
        grad = inverse * (dn[i] * gamma - first - scaled * second) + wpad[i + 1].astype(F32)
        df[0, i] = grad.astype(BF16)
        return carry

    lax.fori_loop(0, ROWS, finish, 0)
    for copy in g1:
        copy.wait_recv()
    total = gx[0, 0]
    for n in range(1, 8):
        total = total + gx[n // 4, n % 4]
    gc[...] = total
    g3 = remote(gc, gcr, g_send.at[7], g_recv.at[7], on_core)
    g3.start()

    x_copy(2).wait_send()
    for s in (2, 3):
        for d in (1, 2, 3):
            y_copy(s, d).wait_send()
            z_copy(s, d).wait_send()
    for copy in sb_copies:
        copy.wait_send()

    for part in (1, 0, 2):
        assemble(core, part, 0, 0)
    for dz, dx in order:
        for part in (1, 0, 2):
            gat_copy(part, dz, dx).wait_recv()
            mate_gat(part, dz, dx).start()
    for dz, dx in order:
        for part in (1, 0, 2):
            assemble(core, part, dz, dx)
    for i in range(4):
        for d in (1, 2, 3):
            a2_copy(i, d).wait_send()
            b2_copy(i, d).wait_send()
        if i < 3:
            c2_copy(i).wait_send()
    for d in (1, 2, 3):
        a3_copy(d).wait_send()
        b3_copy(d).wait_send()
        c3_copy(d).wait_send()
    for copy in g1:
        copy.wait_send()
    for part in range(3):
        for dz, dx in order:
            gat_copy(part, dz, dx).wait_send()
    for dz, dx in ((0, 0),) + order:
        for part in (1, 0, 2):
            mate_gat(part, dz, dx).wait_recv()
            assemble(mate, part, dz, dx)
    g3.wait_recv()
    dg_ref[...] = gc[...] + gcr[...]

    for part in range(3):
        mate_gat(part, 0, 0).wait_send()
        for dz, dx in order:
            mate_gat(part, dz, dx).wait_send()
    g3.wait_send()


def shards(features, cotangent, mask, conv_weight, gamma, beta):
    anywhere = pl.BlockSpec(memory_space=pl.ANY)
    vmem = pl.BlockSpec(memory_space=pltpu.VMEM)
    dma = pltpu.SemaphoreType.DMA

    def buf(*shape, dtype=BF16):
        return pltpu.VMEM(shape, dtype)

    panel = (CI, 128)
    dfeatures, dweight, dgains = pl.pallas_call(
        kernel,
        out_shape=(
            buf(1, ROWS, W, C),
            buf(5, 9 * CI + 8, 128, dtype=F32),
            buf(2, C, dtype=F32),
        ),
        in_specs=[anywhere] * 6,
        out_specs=(vmem, vmem, vmem),
        scratch_shapes=[
            buf(ROWS, W, dtype=jnp.int32),
            buf(C, dtype=F32),
            buf(C, dtype=F32),
            buf(ROWS, W, C),
            buf(ROWS, W, C),
            buf(ROWS + 2, W, C),
            buf(ROWS + 2, W, C),
            buf(CELLS + 2 * W, LANES),
            buf(CELLS + 2 * W, HALF),
            buf(C, K9),
            buf(C, CELLS),
            buf(C, CELLS),
            buf(ROWS, W, C, dtype=F32),
            buf(2, 2, 4, *panel, dtype=F32),
            buf(4, 2, 2, *panel, dtype=F32),
            buf(4, 4, *panel, dtype=F32),
            buf(3, 4, 2, 2, 4, *panel),
            buf(3, 2, 2, 4, *panel),
            buf(3, 4, 2, 2, *panel),
            buf(3, 4, 4, *panel),
            buf(2, 2, 4, *panel, dtype=F32),
            buf(4, 2, 2, *panel, dtype=F32),
            buf(4, 4, *panel, dtype=F32),
            buf(2, 2, 4, *panel),
            buf(4, 2, 2, *panel),
            buf(4, 4, *panel),
            buf(3, 4, *panel),
            buf(3, 4, *panel),
            buf(3, 4, *panel),
            buf(2, 2, *panel, dtype=F32),
            buf(4, *panel, dtype=F32),
            buf(4, *panel, dtype=F32),
            buf(3, 3, *panel, dtype=F32),
            buf(2, 2, 4, 3, *panel),
            buf(STRIPS, 2, C, dtype=F32),
            buf(STRIPS, 2, C, dtype=F32),
            buf(2, 4, 2, C, dtype=F32),
            buf(2, C, dtype=F32),
            buf(2, C, dtype=F32),
            dma((5,)),
            dma((9,)),
            dma((7,)),
            dma((7,)),
            dma((7,)),
            dma((7,)),
            dma((2,)),
            dma((2,)),
            dma((1,)),
            dma((1,)),
            dma((ROWS,)),
            dma((ROWS,)),
            dma((2,)),
            dma((2,)),
            dma((3,)),
            dma((3,)),
            dma((4, 3)),
            dma((4, 3)),
            dma((4, 3)),
            dma((4, 3)),
            dma((4, 3)),
            dma((4, 3)),
            dma((4, 3)),
            dma((4, 3)),
            dma((3,)),
            dma((3,)),
            dma((3, 3)),
            dma((3, 3)),
            dma((3, 8)),
            dma((3, 8)),
            dma((3, 8)),
            dma((3, 8)),
            dma((8,)),
            dma((8,)),
        ],
        compiler_params=pltpu.CompilerParams(
            collective_id=0, has_side_effects=True, vmem_limit_bytes=56 * 1024 * 1024
        ),
        cost_estimate=pl.CostEstimate(flops=4 * CELLS * K9 * C, bytes_accessed=13_000_000, transcendentals=CELLS * C),
    )(features, cotangent, mask, conv_weight, gamma, beta)
    return dfeatures, jnp.concatenate([dweight[j, : 9 * CI] for j in range(5)], axis=1), dgains


def solution(mesh):
    placed = (
        P("dp", "tile", None, None),
        P("dp", "tile", None, None),
        P("dp", "tile", None),
        P(),
        P(),
        P(),
    )
    return jax.shard_map(
        shards,
        mesh=mesh,
        in_specs=placed,
        out_specs=(P("dp", "tile", None, None), P("tile", None), P()),
        check_vma=False,
    )
```

```python
import jax
import jax.numpy as jnp
from jax import lax
from jax.experimental import pallas as pl
from jax.experimental.pallas import tpu as pltpu
from jax.sharding import PartitionSpec as P

MESH = pl.DeviceIdType.MESH
BF16 = jnp.bfloat16
F32 = jnp.float32

G = 32
EPSILON = 1e-05
C = 640
PER_GROUP = C // G
ROWS = 8
W = 128
CELLS = ROWS * W
STRIPS = 8
K3 = 3 * C
LANES = 2048
HALF = LANES // 2
BLOCKS = K3 // 128
K9 = 9 * C
CI = C // STRIPS
COUNT = float(ROWS * STRIPS * W * PER_GROUP)
SUB = 512


def kernel(
    x_hbm, cot_hbm, mask_hbm, w_hbm, gamma_hbm, beta_hbm,
    df, dwv, dg_ref,
    mask_ref, gamma_ref, beta_ref, x, cot, wpad, wpad_m, cols, cols_m, wmat, act_t, act_m, dn,
    part_sum, own1, own2, s1, r1a, r1b, r1c, t2a, t2b, t2c, h2a, h2b, h2c, r2a, r2b, r2c, t3a, t3b, t3c, r3, gat,
    st, sb, gx, gc, gcr,
    load_sem, w_sem,
    st_send, st_recv, sb_send, sb_recv, halo_send, halo_recv,
    wm_send, wm_recv, am_send, am_recv, hm_send, hm_recv,
    a1_send, a1_recv, b1_send, b1_recv, c1_send, c1_recv,
    a2_send, a2_recv, b2_send, b2_recv, c2_send, c2_recv, s3_send, s3_recv,
    gat_send, gat_recv, fwd_send, fwd_recv, g_send, g_recv,
):
    dp = lax.axis_index("dp")
    tile = lax.axis_index("tile")
    core = lax.rem(dp, 2)
    mx = lax.rem(lax.div(dp, 2), 4)
    zlo = lax.div(dp, 8)
    zhi = lax.div(tile, 4)
    my = lax.rem(tile, 4)
    mz = zhi * 2 + zlo
    mate = 1 - core

    def place(px, py, pz, pc):
        return {
            "dp": (lax.rem(pz, 2) * 4 + px) * 2 + pc,
            "tile": lax.div(pz, 2) * 4 + py,
        }

    def x_peer(d):
        return lax.rem(mx + d, 4)

    def y_peer(d):
        return lax.rem(my + d, 4)

    def z_peer(d):
        return lax.rem(mz + d, 4)

    def remote(src, dst, send, recv, device):
        return pltpu.make_async_remote_copy(
            src_ref=src, dst_ref=dst, send_sem=send, recv_sem=recv, device_id=device, device_id_type=MESH
        )

    on_x = [place(x_peer(d), my, mz, core) for d in (1, 2, 3)]
    on_y = [place(mx, y_peer(d), mz, core) for d in (1, 2, 3)]
    on_z = [place(mx, my, z_peer(d), core) for d in (1, 2, 3)]
    on_core = place(mx, my, mz, mate)

    def on_tile(d):
        return {"dp": dp, "tile": lax.rem(tile + d, STRIPS)}

    load_x = pltpu.make_async_copy(x_hbm.at[0], x, load_sem.at[0])
    load_x.start()
    load_cot = pltpu.make_async_copy(cot_hbm.at[0], cot, load_sem.at[1])
    load_cot.start()
    load_mask = pltpu.make_async_copy(mask_hbm.at[0], mask_ref, load_sem.at[2])
    load_gamma = pltpu.make_async_copy(gamma_hbm, gamma_ref, load_sem.at[3])
    load_beta = pltpu.make_async_copy(beta_hbm, beta_ref, load_sem.at[4])
    for load in (load_mask, load_gamma, load_beta):
        load.start()
    loads_w = [
        pltpu.make_async_copy(w_hbm.at[k // 3, k % 3], wmat.at[:, k * C : (k + 1) * C], w_sem.at[k]) for k in range(9)
    ]

    barrier = pltpu.get_barrier_semaphore()
    for device in on_x + on_y + on_z + [on_core]:
        pl.semaphore_signal(barrier, inc=1, device_id=device, device_id_type=MESH)
    for d in (1, 2, 3):
        other = place(mx, y_peer(d), (1 - zhi) * 2 + zlo, core)
        pl.semaphore_signal(barrier, inc=1, device_id=other, device_id_type=MESH)
        other = place(x_peer(d), my, zhi * 2 + 1 - zlo, core)
        pl.semaphore_signal(barrier, inc=1, device_id=other, device_id_type=MESH)

    load_x.wait()

    def fold(value):
        return jnp.sum(value.reshape(W // 8, 8, C), axis=0)

    zeros8 = jnp.zeros((8, C), F32)
    total = lax.fori_loop(0, ROWS, lambda i, acc: acc + fold(x[i].astype(F32)), zeros8)
    total = jnp.sum(total, axis=0, keepdims=True)
    local_mean = total * (1.0 / CELLS)

    def add_squares(i, acc):
        centered = x[i].astype(F32) - local_mean
        return acc + fold(centered * centered)

    squares = jnp.sum(lax.fori_loop(0, ROWS, add_squares, zeros8), axis=0, keepdims=True)
    st[tile, 0:1] = total
    st[tile, 1:2] = squares
    pl.semaphore_wait(barrier, 16)
    st_copies = [remote(st.at[tile], st.at[tile], st_send.at[d - 1], st_recv.at[d - 1], on_tile(d)) for d in range(1, 8)]
    for copy in st_copies:
        copy.start()

    load_cot.wait()
    for load in (load_mask, load_gamma, load_beta):
        load.wait()
    for load in loads_w:
        load.start()
    factor = (1.0 + mask_ref[...].astype(F32)).T
    for i in range(ROWS):
        wpad[i + 1] = (cot[i].astype(F32) * factor[:, i : i + 1]).astype(BF16)
    halo = [
        remote(wpad.at[ROWS], wpad.at[0], halo_send.at[0], halo_recv.at[0], on_tile(1)),
        remote(wpad.at[1], wpad.at[ROWS + 1], halo_send.at[1], halo_recv.at[1], on_tile(7)),
    ]
    mate_w = remote(wpad.at[pl.ds(1, ROWS)], wpad_m.at[pl.ds(1, ROWS)], wm_send.at[0], wm_recv.at[0], on_core)
    mate_w.start()
    for copy in halo:
        copy.start()

    rowsw = lax.broadcasted_iota(jnp.int32, (W, C), 0)

    def shifts(value):
        value = value.astype(F32)
        ahead = jnp.where(rowsw == W - 1, 0.0, pltpu.roll(value, W - 1, 0))
        behind = jnp.where(rowsw == 0, 0.0, pltpu.roll(value, 1, 0))
        return ahead.astype(BF16), value.astype(BF16), behind.astype(BF16)

    def spread(r):
        rows = pl.ds(pl.multiple_of(r * W, W), W)
        for ox, shifted in enumerate(shifts(wpad[r])):
            cols[rows, ox * C : (ox + 1) * C] = shifted
        cols[rows, K3:] = jnp.zeros((W, LANES - K3), BF16)

    def spread_mate(r):
        rows = pl.ds(pl.multiple_of(r * W, W), W)
        ahead, middle, behind = shifts(wpad_m[r])
        split = HALF - C

        @pl.when(core == 0)
        def _():
            cols_m[rows, :C] = ahead
            cols_m[rows, C:] = middle[:, :split]

        @pl.when(core == 1)
        def _():
            cols_m[rows, : C - split] = middle[:, split:]
            cols_m[rows, C - split : 2 * C - split] = behind
            cols_m[rows, 2 * C - split :] = jnp.zeros((W, LANES - K3), BF16)

    def inner(step):
        def body(r, carry):
            step(r)
            return carry

        lax.fori_loop(1, ROWS + 1, body, 0)

    inner(spread)

    chan = lax.broadcasted_iota(jnp.int32, (C, 128), 0).astype(F32)
    group = lax.broadcasted_iota(jnp.int32, (C, 128), 1).astype(F32)
    member = jnp.where(jnp.floor((chan + 0.5) * (1.0 / PER_GROUP)) == group, 1.0, 0.0).astype(BF16)
    chan_t = lax.broadcasted_iota(jnp.int32, (128, C), 1).astype(F32)
    group_t = lax.broadcasted_iota(jnp.int32, (128, C), 0).astype(F32)
    member_t = jnp.where(jnp.floor((chan_t + 0.5) * (1.0 / PER_GROUP)) == group_t, 1.0, 0.0).astype(BF16)

    def in_parts(value):
        high = value.astype(BF16).astype(F32)
        middle = (value - high).astype(BF16).astype(F32)
        return jnp.concatenate([high, middle, value - high - middle], axis=0).astype(BF16)

    def times(value, table):
        product = jnp.dot(in_parts(value), table, preferred_element_type=F32)
        return product[0:8] + product[8:16] + product[16:24]

    def to_groups(value):
        return times(value, member)

    def to_channels(value):
        return times(value, member_t)

    for copy in st_copies:
        copy.wait_recv()
    sums = st[0]
    for i in range(1, STRIPS):
        sums = sums + st[i]
    mean = to_channels(to_groups(jnp.broadcast_to(sums[0:1], (8, C))) * (1.0 / COUNT))[0:1]
    apart = jnp.zeros((1, C), F32)
    for i in range(STRIPS):
        centered = st[i, 0:1] * (1.0 / CELLS) - mean
        apart = apart + centered * centered
    spread_sq = apart * float(CELLS) + sums[1:2]
    variance = to_groups(jnp.broadcast_to(spread_sq, (8, C))) * (1.0 / COUNT)
    inverse = to_channels(lax.rsqrt(variance + EPSILON))[0:1]
    gamma = gamma_ref[...].reshape(1, C)
    beta = beta_ref[...].reshape(1, C)

    def mate_act(i):
        block = pl.ds(pl.multiple_of(i * W, W), W)
        return remote(act_t.at[:, block], act_m.at[:, block], am_send.at[i], am_recv.at[i], on_core)

    def activate(i, carry):
        scaled = (x[i].astype(F32) - mean) * inverse
        normed = scaled * gamma + beta
        sig = 0.5 + 0.5 * jnp.tanh(0.5 * normed)
        act = normed * sig
        dn[i] = sig * (1.0 + normed * (1.0 - sig))
        act_t[:, pl.ds(pl.multiple_of(i * W, W), W)] = act.T.astype(BF16)
        mate_act(i).start()
        return carry

    lax.fori_loop(0, ROWS, activate, 0)

    for copy in halo:
        copy.wait_recv()

    @pl.when(tile == 0)
    def _():
        wpad[0] = jnp.zeros((W, C), BF16)

    @pl.when(tile == STRIPS - 1)
    def _():
        wpad[ROWS + 1] = jnp.zeros((W, C), BF16)

    mate_edge = [
        remote(wpad.at[r], wpad_m.at[r], hm_send.at[n], hm_recv.at[n], on_core) for n, r in enumerate((0, ROWS + 1))
    ]
    for copy in mate_edge:
        copy.start()
    spread(0)
    spread(ROWS + 1)
    mate_w.wait_recv()
    inner(spread_mate)
    for copy in mate_edge:
        copy.wait_recv()
    spread_mate(0)
    spread_mate(ROWS + 1)
    for i in range(ROWS):
        mate_act(i).wait_recv()

    def partial(part, xq):
        rows = pl.ds((2 - part) * W, CELLS)
        own = cols[rows, pl.ds(pl.multiple_of(core * HALF + xq * 256, 256), 256)]
        theirs = cols_m[rows, pl.ds(pl.multiple_of(xq * 256, 256), 256)]
        return jnp.dot(act_t[...], own, preferred_element_type=F32) + jnp.dot(
            act_m[...], theirs, preferred_element_type=F32
        )

    def turn(s):
        return jnp.where(s == 0, 2, jnp.where(s == 1, 1, jnp.where(s == 2, 3, 0)))

    def x_copy(s):
        xq = x_peer(turn(s))
        return remote(s1.at[0, xq], r1a.at[s], a1_send.at[s], a1_recv.at[s], place(xq, my, mz, core))

    def y_copy(s, d):
        xq = x_peer(turn(s))
        src = s1.at[1, xq, :, :, y_peer(d)]
        return remote(src, r1b.at[d - 1, xq], b1_send.at[s, d - 1], b1_recv.at[s, d - 1], on_y[d - 1])

    def z_copy(s, d):
        xq = x_peer(turn(s))
        src = s1.at[2, xq, lax.rem(z_peer(d), 2), lax.div(z_peer(d), 2)]
        return remote(src, r1c.at[d - 1, xq], c1_send.at[s, d - 1], c1_recv.at[s, d - 1], on_z[d - 1])

    def grad_step(s, carry):
        xq = x_peer(turn(s))
        for part in range(3):
            result = partial(part, xq)
            for b in range(2):
                piece = result[:, b * 128 : (b + 1) * 128].reshape(2, 4, CI, 128)
                part_sum[b] = piece
                s1[part, xq, b] = piece.astype(BF16)
            if part == 0:

                @pl.when(s < 3)
                def _():
                    x_copy(s).start()

            for d in (1, 3, 2):
                if part == 1:
                    y_copy(s, d).start()
                if part == 2:
                    z_copy(s, d).start()
            if part == 1:
                own1[xq] = part_sum[:, :, my]
            if part == 2:
                own2[xq] = part_sum[zlo, zhi]
            if part == 0:

                @pl.when(s == 3)
                def _():
                    t2a[...] = part_sum[...]
        return carry

    lax.fori_loop(0, 4, grad_step, 0)

    for load in loads_w:
        load.wait()

    def dactive_step(i, carry):
        s0, s1_ = carry
        dact = jnp.zeros((SUB, C), F32)
        for oy in range(3):
            window = cols[pl.ds(pl.multiple_of(i * SUB + (2 - oy) * W, W), SUB), :K3]
            dact = dact + lax.dot_general(
                window, wmat[:, oy * K3 : (oy + 1) * K3], (((1,), (1,)), ((), ())), preferred_element_type=F32
            )
        for j in range(SUB // W):
            r = i * (SUB // W) + j
            dnormed = dact[j * W : (j + 1) * W] * dn[r]
            dn[r] = dnormed
            scaled = (x[r].astype(F32) - mean) * inverse
            s0 = s0 + fold(dnormed)
            s1_ = s1_ + fold(dnormed * scaled)
        return s0, s1_

    def z_of(d):
        return lax.rem(z_peer(d), 2), lax.div(z_peer(d), 2)

    def b2_copy(i, d):
        xq = x_peer(turn(i))
        zq, zh = z_of(d)
        return remote(h2b.at[xq, zq, zh], r2b.at[d - 1, xq], b2_send.at[i, d - 1], b2_recv.at[i, d - 1], on_z[d - 1])

    def c2_copy(i):
        xq = x_peer(turn(i))
        return remote(h2c.at[xq], r2c.at[i], c2_send.at[i], c2_recv.at[i], place(xq, my, mz, core))

    def a2_copy(n, d):
        zq, zh = z_of(n)
        return remote(h2a.at[zq, zh, y_peer(d)], r2a.at[d - 1, n], a2_send.at[n, d - 1], a2_recv.at[n, d - 1], on_y[d - 1])

    def a3_copy(d):
        zq, zh = z_of(d)
        return remote(t3a.at[zq, zh], r3.at[0, d - 1], s3_send.at[0, d - 1], s3_recv.at[0, d - 1], on_z[d - 1])

    def b3_copy(d):
        return remote(t3b.at[x_peer(d)], r3.at[1, d - 1], s3_send.at[1, d - 1], s3_recv.at[1, d - 1], on_x[d - 1])

    def c3_copy(d):
        return remote(t3c.at[y_peer(d)], r3.at[2, d - 1], s3_send.at[2, d - 1], s3_recv.at[2, d - 1], on_y[d - 1])

    def first_bc(i):
        xq = x_peer(turn(i))
        for d in (1, 2, 3):
            y_copy(i, d).wait_recv()
        total = own1[xq] + r1b[0, xq].astype(F32) + r1b[1, xq].astype(F32) + r1b[2, xq].astype(F32)
        t2b[xq] = total
        h2b[xq] = total.astype(BF16)
        for d in (1, 3, 2):
            b2_copy(i, d).start()
        for d in (1, 2, 3):
            z_copy(i, d).wait_recv()
        total = own2[xq] + r1c[0, xq].astype(F32) + r1c[1, xq].astype(F32) + r1c[2, xq].astype(F32)
        t2c[xq] = total
        h2c[xq] = total.astype(BF16)
        if i < 3:
            c2_copy(i).start()

    def first_sent(s):
        mate_act(s * 4).wait_send()
        mate_act(s * 4 + 1).wait_send()
        mate_act(s * 4 + 2).wait_send()
        mate_act(s * 4 + 3).wait_send()
        x_copy(s).wait_send()
        for d in (1, 2, 3):
            y_copy(s, d).wait_send()
            z_copy(s, d).wait_send()

    def first_a():
        for i in range(3):
            x_copy(i).wait_recv()
        total = t2a[...] + r1a[0].astype(F32) + r1a[1].astype(F32) + r1a[2].astype(F32)
        t2a[...] = total
        h2a[...] = total.astype(BF16)
        for n in (1, 3, 2, 0):
            for d in (1, 3, 2):
                a2_copy(n, d).start()

    sums01 = (zeros8, zeros8)
    sums01 = dactive_step(0, sums01)
    first_bc(0)
    first_bc(1)
    for copy in st_copies + halo + [mate_w] + mate_edge:
        copy.wait_send()
    for s in range(2):
        first_sent(s)
    first_a()
    first_bc(2)
    first_bc(3)
    sums01 = dactive_step(1, sums01)
    sum0 = jnp.sum(sums01[0], axis=0, keepdims=True)
    sum1 = jnp.sum(sums01[1], axis=0, keepdims=True)
    sb[tile, 0:1] = sum1
    sb[tile, 1:2] = sum0
    sb_copies = [remote(sb.at[tile], sb.at[tile], sb_send.at[d - 1], sb_recv.at[d - 1], on_tile(d)) for d in range(1, 8)]
    for copy in sb_copies:
        copy.start()

    for i, n in ((0, 2), (1, 1), (2, 3), (3, 0)):
        xq = x_peer(n)
        for d in (1, 2, 3):
            b2_copy(i, d).wait_recv()
        t3b[xq] = (
            t2b[xq, zlo, zhi] + r2b[0, xq].astype(F32) + r2b[1, xq].astype(F32) + r2b[2, xq].astype(F32)
        )
        if n:
            b3_copy(n).start()
        zq, zh = z_of(n)
        for d in (1, 2, 3):
            a2_copy(n, d).wait_recv()
        t3a[zq, zh] = (
            t2a[zq, zh, my] + r2a[0, n].astype(F32) + r2a[1, n].astype(F32) + r2a[2, n].astype(F32)
        )
        if n:
            a3_copy(n).start()
    for i in range(3):
        c2_copy(i).wait_recv()
    t3c[...] = t2c[mx] + r2c[0].astype(F32) + r2c[1].astype(F32) + r2c[2].astype(F32)
    for d in (1, 3, 2):
        c3_copy(d).start()

    order = ((0, 1), (0, 3), (1, 0), (0, 2), (1, 1), (1, 3), (1, 2))

    for copy in sb_copies:
        copy.wait_recv()
    gsum = sb[0]
    for i in range(1, STRIPS):
        gsum = gsum + sb[i]
    gx[zlo, mx] = gsum
    g1 = []
    for n, (dz, dx) in enumerate(order):
        target = place(x_peer(dx), my, zhi * 2 + lax.rem(zlo + dz, 2), core)
        g1.append(remote(gx.at[zlo, mx], gx.at[zlo, mx], g_send.at[n], g_recv.at[n], target))
    for copy in g1:
        copy.start()


    def gat_copy(part, dz, dx):
        mine = gat.at[core, zlo, mx, part]
        target = place(x_peer(dx), my, zhi * 2 + lax.rem(zlo + dz, 2), core)
        return remote(mine, mine, gat_send.at[part, dz * 4 + dx], gat_recv.at[part, dz * 4 + dx], target)

    def mate_gat(part, dz, dx):
        block = gat.at[core, lax.rem(zlo + dz, 2), lax.rem(mx + 4 - dx, 4), part]
        return remote(block, block, fwd_send.at[part, dz * 4 + dx], fwd_recv.at[part, dz * 4 + dx], on_core)

    def assemble(c, part, dz, dx):
        zq = lax.rem(zlo + dz, 2)
        xq = lax.rem(mx + 4 - dx, 4)
        b = c * 8 + xq * 2 + zq

        @pl.when(b < BLOCKS)
        def _():
            k = part * 3 + lax.div(b, 5)
            j = lax.rem(b, 5)
            dwv[j, pl.ds(k, CI, stride=9), :] = gat[c, zq, xq, part].astype(F32)

    for part, third in ((1, b3_copy), (0, a3_copy), (2, c3_copy)):
        for d in (1, 2, 3):
            third(d).wait_recv()
        own = (t3a[zlo, zhi], t3b[mx], t3c[my])[part]
        gat[core, zlo, mx, part] = (own + r3[part, 0] + r3[part, 1] + r3[part, 2]).astype(BF16)
        for dz, dx in order:
            gat_copy(part, dz, dx).start()
        mate_gat(part, 0, 0).start()

    weighed = gsum * gamma
    row8 = lax.broadcasted_iota(jnp.int32, (8, C), 0)
    weighed = jnp.where(row8 == 0, weighed[0:1], weighed[1:2])
    moments = to_channels(to_groups(weighed) * (1.0 / COUNT))
    second = moments[0:1]
    first = moments[1:2]

    def finish(i, carry):
        scaled = (x[i].astype(F32) - mean) * inverse
        grad = inverse * (dn[i] * gamma - first - scaled * second) + wpad[i + 1].astype(F32)
        df[0, i] = grad.astype(BF16)
        return carry

    lax.fori_loop(0, ROWS, finish, 0)
    for copy in g1:
        copy.wait_recv()
    total = gx[0, 0]
    for n in range(1, 8):
        total = total + gx[n // 4, n % 4]
    gc[...] = total
    g3 = remote(gc, gcr, g_send.at[7], g_recv.at[7], on_core)
    g3.start()

    x_copy(2).wait_send()
    for s in (2, 3):
        for d in (1, 2, 3):
            y_copy(s, d).wait_send()
            z_copy(s, d).wait_send()
    for copy in sb_copies:
        copy.wait_send()

    for part in (1, 0, 2):
        assemble(core, part, 0, 0)
    for dz, dx in order:
        for part in (1, 0, 2):
            gat_copy(part, dz, dx).wait_recv()
            mate_gat(part, dz, dx).start()
    for dz, dx in order:
        for part in (1, 0, 2):
            assemble(core, part, dz, dx)
    for i in range(4):
        for d in (1, 2, 3):
            a2_copy(i, d).wait_send()
            b2_copy(i, d).wait_send()
        if i < 3:
            c2_copy(i).wait_send()
    for d in (1, 2, 3):
        a3_copy(d).wait_send()
        b3_copy(d).wait_send()
        c3_copy(d).wait_send()
    for copy in g1:
        copy.wait_send()
    for part in range(3):
        for dz, dx in order:
            gat_copy(part, dz, dx).wait_send()
    for dz, dx in ((0, 0),) + order:
        for part in (1, 0, 2):
            mate_gat(part, dz, dx).wait_recv()
            assemble(mate, part, dz, dx)
    g3.wait_recv()
    dg_ref[...] = gc[...] + gcr[...]

    for part in range(3):
        mate_gat(part, 0, 0).wait_send()
        for dz, dx in order:
            mate_gat(part, dz, dx).wait_send()
    g3.wait_send()


def shards(features, cotangent, mask, conv_weight, gamma, beta):
    anywhere = pl.BlockSpec(memory_space=pl.ANY)
    vmem = pl.BlockSpec(memory_space=pltpu.VMEM)
    dma = pltpu.SemaphoreType.DMA

    def buf(*shape, dtype=BF16):
        return pltpu.VMEM(shape, dtype)

    panel = (CI, 128)
    dfeatures, dweight, dgains = pl.pallas_call(
        kernel,
        out_shape=(
            buf(1, ROWS, W, C),
            buf(5, 9 * CI + 8, 128, dtype=F32),
            buf(2, C, dtype=F32),
        ),
        in_specs=[anywhere] * 6,
        out_specs=(vmem, vmem, vmem),
        scratch_shapes=[
            buf(ROWS, W, dtype=jnp.int32),
            buf(C, dtype=F32),
            buf(C, dtype=F32),
            buf(ROWS, W, C),
            buf(ROWS, W, C),
            buf(ROWS + 2, W, C),
            buf(ROWS + 2, W, C),
            buf(CELLS + 2 * W, LANES),
            buf(CELLS + 2 * W, HALF),
            buf(C, K9),
            buf(C, CELLS),
            buf(C, CELLS),
            buf(ROWS, W, C, dtype=F32),
            buf(2, 2, 4, *panel, dtype=F32),
            buf(4, 2, 2, *panel, dtype=F32),
            buf(4, 4, *panel, dtype=F32),
            buf(3, 4, 2, 2, 4, *panel),
            buf(3, 2, 2, 4, *panel),
            buf(3, 4, 2, 2, *panel),
            buf(3, 4, 4, *panel),
            buf(2, 2, 4, *panel, dtype=F32),
            buf(4, 2, 2, *panel, dtype=F32),
            buf(4, 4, *panel, dtype=F32),
            buf(2, 2, 4, *panel),
            buf(4, 2, 2, *panel),
            buf(4, 4, *panel),
            buf(3, 4, *panel),
            buf(3, 4, *panel),
            buf(3, 4, *panel),
            buf(2, 2, *panel, dtype=F32),
            buf(4, *panel, dtype=F32),
            buf(4, *panel, dtype=F32),
            buf(3, 3, *panel, dtype=F32),
            buf(2, 2, 4, 3, *panel),
            buf(STRIPS, 2, C, dtype=F32),
            buf(STRIPS, 2, C, dtype=F32),
            buf(2, 4, 2, C, dtype=F32),
            buf(2, C, dtype=F32),
            buf(2, C, dtype=F32),
            dma((5,)),
            dma((9,)),
            dma((7,)),
            dma((7,)),
            dma((7,)),
            dma((7,)),
            dma((2,)),
            dma((2,)),
            dma((1,)),
            dma((1,)),
            dma((ROWS,)),
            dma((ROWS,)),
            dma((2,)),
            dma((2,)),
            dma((3,)),
            dma((3,)),
            dma((4, 3)),
            dma((4, 3)),
            dma((4, 3)),
            dma((4, 3)),
            dma((4, 3)),
            dma((4, 3)),
            dma((4, 3)),
            dma((4, 3)),
            dma((3,)),
            dma((3,)),
            dma((3, 3)),
            dma((3, 3)),
            dma((3, 8)),
            dma((3, 8)),
            dma((3, 8)),
            dma((3, 8)),
            dma((8,)),
            dma((8,)),
        ],
        compiler_params=pltpu.CompilerParams(
            collective_id=0, has_side_effects=True, vmem_limit_bytes=56 * 1024 * 1024
        ),
        cost_estimate=pl.CostEstimate(flops=4 * CELLS * K9 * C, bytes_accessed=13_000_000, transcendentals=CELLS * C),
    )(features, cotangent, mask, conv_weight, gamma, beta)
    return dfeatures, jnp.concatenate([dweight[j, : 9 * CI] for j in range(5)], axis=1), dgains


def solution(mesh):
    placed = (
        P("dp", "tile", None, None),
        P("dp", "tile", None, None),
        P("dp", "tile", None),
        P(),
        P(),
        P(),
    )
    return jax.shard_map(
        shards,
        mesh=mesh,
        in_specs=placed,
        out_specs=(P("dp", "tile", None, None), P("tile", None), P()),
        check_vma=False,
    )
```
